512 devices in a mesh: section: 8 (over x, core), tm: 64 (over y, z).
Axes of the slice: x: 4, y: 4, z: 16, core: 2. Of those that a mesh axis runs over, the one named last changes fastest.
Arguments:
- signal: bfloat16 [2, 16384, 128], P(None, 'tm'), may hold values from -6 to 6
- conv_weight: bfloat16 [8, 5, 384, 256], P('section'), may hold values from -0.3125 to 0.3125
- conv_bias: float32 [8, 5, 256], P('section'), may hold values from -3 to 3
- out_weight: bfloat16 [8, 5, 128, 256], P('section'), may hold values from -0.5 to 0.5
- out_bias: float32 [8, 5, 256], P('section'), may hold values from -3 to 3
Outputs:
- boundary_res: bfloat16 [8, 2, 16384, 128], P('section', None, 'tm')
- boundary_skip: float32 [8, 2, 16384, 128], P('section', None, 'tm')
The draws below stay inside these ranges and needn't reach their ends.
All inputs are finite; a program needn't handle non-finite values.
Results may differ from the reference program's by a relative error of at most 0.028.
Values may be sent and summed in bfloat16 or wider, within the bound.
A program may use at most 64 MiB of HBM per device.

```python
import jax
import jax.numpy as jnp

C = 128
L_SECTION = 5
T_DEV = 256
MICRO = 2
TIME = 16384
N_SECTION = 8


def block_levels(stream_key, extent, pieces, least, top_value):
    factor_of, own = 1.0, jax.random.fold_in(stream_key, 6)
    for dim, shards_of in pieces:
        heights = jnp.exp(jax.random.uniform(jax.random.fold_in(own, dim), (shards_of,), jnp.float32, least / len(pieces), top_value / len(pieces)))
        factor_of = factor_of * jnp.repeat(heights, extent[dim] // shards_of).reshape([-1 if axis == dim else 1 for axis in range(len(extent))])
    return factor_of


def centred(key, extent, spread, limit, shards=(), held_as=jnp.bfloat16):
    result = jax.random.normal(key, extent, jnp.float32) * spread
    if len(shards) > 0:
        result = block_levels(key, extent, shards, -0.22, 0.18) * result
    return jnp.clip(result, min=-limit, max=limit).astype(held_as)


def setup_inputs(seed: int = 0) -> dict:
    streams_of = jax.random.split(jax.random.key(seed), 6)
    return {
        "signal": centred(streams_of[0], (MICRO, TIME, C), 1.0, 6.0, ((1, 64),)),
        "conv_weight": centred(streams_of[1], (N_SECTION, L_SECTION, 3 * C, 2 * C), (3 * C) ** -0.5, 0.3125, ((0, 8),)),
        "conv_bias": centred(streams_of[2], (N_SECTION, L_SECTION, 2 * C), 0.5, 3.0, ((0, 8),), jnp.float32),
        "out_weight": centred(streams_of[3], (N_SECTION, L_SECTION, C, 2 * C), C ** -0.5, 0.5, ((0, 8),)),
        "out_bias": centred(streams_of[4], (N_SECTION, L_SECTION, 2 * C), 0.5, 3.0, ((0, 8),), jnp.float32),
    }


def delayed(values, lag):
    zeros = jnp.zeros((lag, values.shape[1]), values.dtype)
    return jnp.concatenate([zeros, values[:-lag]], axis=0)


def one_layer(state, skip, conv_w, conv_b, out_w, out_b, lag):
    width = state.shape[1]
    inputs = state.astype(jnp.bfloat16)
    stacked = jnp.concatenate([delayed(inputs, 2 * lag), delayed(inputs, lag), inputs], axis=1)
    pre = jnp.dot(stacked, conv_w, preferred_element_type=jnp.float32) + conv_b
    gated = (jnp.tanh(pre[:, :width]) * jax.nn.sigmoid(pre[:, width:])).astype(jnp.bfloat16)
    post = jnp.dot(gated, out_w, preferred_element_type=jnp.float32) + out_b
    return state + post[:, :width], skip + post[:, width:]


def reference(signal, conv_weight, conv_bias, out_weight, out_bias):
    spans = (1, 16, T_DEV // 4, T_DEV // 2, 2 * T_DEV)
    res_all = []
    skip_all = []
    for group in range(N_SECTION):
        res_all.append([])
        skip_all.append([])
    for record in range(MICRO):
        state = signal[record].astype(jnp.float32)
        skip = jnp.zeros(state.shape, jnp.float32)
        for group in range(N_SECTION):
            for layer in range(L_SECTION):
                state, skip = one_layer(state, skip, conv_weight[group, layer], conv_bias[group, layer],
                                        out_weight[group, layer], out_bias[group, layer], spans[layer])
            rounded = state.astype(jnp.bfloat16)
            res_all[group].append(rounded)
            skip_all[group].append(skip)
            state = rounded.astype(jnp.float32)
    boundary_res = jnp.stack([jnp.stack(rows) for rows in res_all])
    boundary_skip = jnp.stack([jnp.stack(rows) for rows in skip_all])
    return boundary_res, boundary_skip
```

```python
import jax
import jax.numpy as jnp
from jax import lax
from jax.experimental import pallas as pl
from jax.experimental.pallas import tpu as pltpu
from jax.sharding import PartitionSpec as P

MESH = pl.DeviceIdType.MESH
C = 128
ROWS = 256
NB = 64
FAR = 176
HALO = FAR + ROWS
SPAN = HALO + ROWS
LAYERS = 5
SPANS = (1, 16, 64, 128, 512)
QUARTER = 64
CUT = 176
EARLY = (CUT, ROWS)
LATE = (0, CUT)
OWN = ((0, 16, ROWS), (1, 48, ROWS), (2, 176, ROWS))
NEAR = ((0, -240, 16), (1, -208, 48), (2, -80, 176), (3, 176, ROWS))
DISTANT = ((0, -416, -240), (1, -384, -208), (2, -256, -80), (3, 0, 176))


def kernel(signal, conv_w, conv_b, out_w, out_b, result,
           wc, wo, bc, bo, ha, h0f, hbuf, xb, xo, xback, hend, sk, skin, made, relay,
           wsend, wsem, a_send, a_sem, r_send, r_sem, init_send, b_send, b_sem, h_send, s_send, s_sem,
           o_send, o_sem, done):
    section = lax.axis_index("section")
    tm = lax.axis_index("tm")
    x, c = section // 2, section % 2
    y, z = tm // 16, tm % 16
    turned = (y + 3 + c) % 4
    pos = z * 4 + (turned ^ (turned >> 1))
    t = jnp.where(c == 1, pos, NB - 1 - pos)
    step = 2 * c - 1

    def tm_of(p, rec):
        n = p % 4
        return (((n ^ (n >> 1)) + 1 - rec) % 4) * 16 + p // 4

    def ahead(k):
        return tm_of((pos + step * k + NB) % NB, c)

    def worker(block, rec):
        return tm_of(jnp.where(rec == 1, block, NB - 1 - block), rec)

    other = 1 - c
    mine = jnp.where(tm == t, 1, 0)

    barrier = pltpu.get_barrier_semaphore()

    def greet(sec, where):
        pl.semaphore_signal(barrier, inc=1, device_id=(sec, where), device_id_type=MESH)

    greet(x * 2 + other, tm)
    for k in (1, 2, 4):
        greet(section, ahead(-k))

    @pl.when(x > 0)
    def _():
        for k in range(3):
            greet(section - 2, ahead(-k))

    greet(x * 2 + other, t)

    @pl.when(x == 0)
    def _():
        for plane in range(4):
            for k in range(3):
                if plane > 0 or k == 1:
                    greet(plane * 2 + c, ahead(-k))

    for m in range(2):
        @pl.when(jnp.logical_or(c != m, tm != worker(tm, m)))
        def _():
            greet(x * 2 + m, worker(tm, m))

    pl.semaphore_wait(barrier, 7 - mine + jnp.where(x < 3, 3, 0) + jnp.where(x == 0, 1, 3))

    def remote(src, dst, send, recv, sec, where):
        return pltpu.make_async_remote_copy(
            src_ref=src, dst_ref=dst, send_sem=send, recv_sem=recv,
            device_id=(sec, where), device_id_type=MESH)

    quarter = remote(signal.at[other, pl.ds(pl.multiple_of(x * QUARTER, QUARTER), QUARTER)], relay, r_send, r_sem,
                     x * 2 + other, worker(tm, other))
    quarter.start()

    parts = (
        ((EARLY, HALO), (LATE, HALO)),
        ((EARLY, FAR), (LATE, FAR)),
        ((EARLY, FAR - ROWS), ((ROWS - FAR, CUT), FAR - ROWS)),
    )

    def start_copies(g, src, sends, sec):
        out = []
        for k in range(3):
            for i, ((lo, hi), base) in enumerate(parts[k]):
                out.append(remote(src.at[pl.ds(lo, hi - lo)], ha.at[g, pl.ds(base + lo, hi - lo)],
                                  sends.at[k, i], a_sem.at[g, k, i if g else 0], sec, ahead(k)))
        return out

    jobs = []
    for layer in range(LAYERS):
        jobs.append((conv_w.at[0, layer], lambda g, l=layer: wc.at[g, l]))
        jobs.append((out_w.at[0, layer], lambda g, l=layer: wo.at[g, l]))
        if layer == 0:
            jobs.append((conv_b, lambda g: bc.at[g]))
            jobs.append((out_b, lambda g: bo.at[g]))
    w_copies = []
    for i, (src, dst) in enumerate(jobs):
        cp = remote(src, dst(c), wsend.at[i], wsem.at[c, i], x * 2 + other, tm)
        cp.start()
        w_copies.append(cp)
        pltpu.make_async_copy(src, dst(c), wsem.at[c, i]).start()
    need = {0: (0, 1, 2, 3), 1: (4, 5), 2: (6, 7), 3: (8, 9), 4: (10, 11)}

    def wait_weights(g, layer):
        for i in need[layer]:
            src, dst = jobs[i]
            pltpu.make_async_copy(src, dst(g), wsem.at[g, i]).wait()

    def dense(taps, g, layer, own):
        pre = jnp.dot(jnp.concatenate(taps, axis=1), wc[g, layer],
                      preferred_element_type=jnp.float32) + bc[g, layer]
        gated = (jnp.tanh(pre[:, :C]) * (0.5 * jnp.tanh(0.5 * pre[:, C:]) + 0.5)).astype(jnp.bfloat16)
        if own:
            return jnp.dot(gated, wo[g, layer], preferred_element_type=jnp.float32) + bo[g, layer]
        return (jnp.dot(gated, wo[g, layer, :, pl.ds(0, C)], preferred_element_type=jnp.float32)
                + bo[g, layer, :, pl.ds(0, C)])

    next_section = jnp.where(x < 3, section + 2, section - 6)
    hand = start_copies(0, hend, h_send, next_section)
    skip_hand = remote(made.at[1, 1], skin, s_send, s_sem, next_section, ahead(0))
    inner = start_copies(1, ha.at[1, pl.ds(HALO, ROWS)], a_send, section)
    b_copies = [[[remote(xo.at[g, pl.ds(lo, hi - lo)], xback.at[g, i, pl.ds(lo, hi - lo)],
                         b_send.at[g, i, j], b_sem.at[g, i, j], section, ahead(k))
                  for i, k in enumerate((2, 4))]
                 for j, (lo, hi) in enumerate((EARLY, LATE))] for g in range(2)]
    away = [jnp.logical_or(c != g, mine == 0) for g in range(2)]
    outs = [(remote(made.at[g], result.at[c], o_send.at[g], o_sem.at[c], x * 2 + g, t),
             pltpu.make_async_copy(made.at[g], result.at[c], o_sem.at[c])) for g in range(2)]

    def send_out(g):
        far, near = outs[g]

        @pl.when(away[g])
        def _():
            far.start()

        @pl.when(jnp.logical_not(away[g]))
        def _():
            near.start()

    def first_rows(k, row, n, start):
        base = (HALO, FAR, FAR - ROWS)[k]
        return remote(relay.at[pl.ds(row, n)], ha.at[0, pl.ds(pl.multiple_of(base + start, 16), n)],
                      init_send.at[k], a_sem.at[0, k, 0], c, ahead(k))

    first = x * QUARTER
    quarter.wait_recv()

    @pl.when(x == 0)
    def _():
        pltpu.make_async_copy(relay, ha.at[0, pl.ds(HALO, QUARTER)], a_sem.at[0, 0, 0]).start()
        first_rows(1, 0, QUARTER, 0).start()

    @pl.when(x > 0)
    def _():
        first_rows(0, 0, QUARTER, first).start()
        first_rows(1, 0, QUARTER, first).start()

    @pl.when(x == 1)
    def _():
        first_rows(2, 16, QUARTER - 16, QUARTER + 16).start()

    @pl.when(x > 1)
    def _():
        first_rows(2, 0, QUARTER, first).start()

    def wait_start(k):
        rows = (pl.ds(HALO, ROWS), pl.ds(FAR, ROWS), pl.ds(0, FAR))[k]
        pltpu.make_async_copy(ha.at[0, rows], ha.at[0, rows], a_sem.at[0, k, 0]).wait()

    seen1 = jnp.where(t >= 1, 1.0, 0.0).astype(jnp.float32)
    seen2 = jnp.where(t >= 2, 1.0, 0.0).astype(jnp.float32)

    def tasks(g, todo):
        for layer, first, last in todo:
            d = SPANS[layer]
            for lo, hi in ((first, last),):
                at, n = lo + HALO, hi - lo
                if layer == 0:
                    taps = [h0f[pl.ds(at - 2, n), :].astype(jnp.bfloat16),
                            h0f[pl.ds(at - 1, n), :].astype(jnp.bfloat16),
                            ha[g, pl.ds(at, n), :]]
                    before = h0f
                else:
                    src = xb.at[layer - 1]
                    taps = [src[pl.ds(at - 2 * d, n), :], src[pl.ds(at - d, n), :], src[pl.ds(at, n), :]]
                    before = hbuf
                post = dense(taps, g, layer, hi > 0)
                h = before[pl.ds(at, n), :] + post[:, :C]
                hbuf[pl.ds(at, n), :] = h
                for begin, end, seen in ((-HALO, -ROWS, seen2), (-ROWS, 0, seen1), (0, ROWS, None)):
                    i, j = max(begin, lo), min(end, hi)
                    if i >= j:
                        continue
                    part = h[i - lo:j - lo]
                    if seen is not None:
                        part = part * seen
                    else:
                        s = post[i - lo:j - lo, C:]
                        if layer > 0 or g > 0:
                            s = s + sk[pl.ds(i, j - i), :]
                        sk[pl.ds(i, j - i), :] = s
                    if layer < 3:
                        xb[layer, pl.ds(i + HALO, j - i), :] = part.astype(jnp.bfloat16)
                    else:
                        xo[g, pl.ds(i, j - i), :] = part.astype(jnp.bfloat16)

    def last_layer(g, j):
        lo, hi = (EARLY, LATE)[j]
        rows = pl.ds(lo, hi - lo)
        for cp in b_copies[g][j]:
            cp.wait_recv()

        @pl.when(t < 4)
        def _():
            xback[g, 1, rows] = jnp.zeros((hi - lo, C), jnp.bfloat16)

        @pl.when(t < 2)
        def _():
            xback[g, 0, rows] = jnp.zeros((hi - lo, C), jnp.bfloat16)

        post = dense([xback[g, 1, rows, :], xback[g, 0, rows, :], xo[g, rows, :]], g, 4, True)
        h = (hbuf[pl.ds(lo + HALO, hi - lo), :] + post[:, :C]).astype(jnp.bfloat16)
        if g == 0:
            ha[1, pl.ds(HALO + lo, hi - lo), :] = h
            for k in (1, 2):
                inner[2 * k + j].start()
        else:
            hend[rows, :] = h

            @pl.when(x < 3)
            def _():
                for k in range(3):
                    hand[2 * k + j].start()
        skip = sk[rows, :] + post[:, C:]
        sk[rows, :] = skip
        made[g, 0, rows, :] = h
        made[g, 1, rows, :] = skip.astype(jnp.bfloat16)

    def widen(g, lo, n):
        h0f[pl.ds(lo, n), :] = ha[g, pl.ds(lo, n), :].astype(jnp.float32)

    for g in range(2):
        def wait_halo(k):
            if g == 0:
                wait_start(k)
            else:
                for cp in inner[2 * k:2 * k + 2]:
                    cp.wait_recv()

        for layer in range(LAYERS - 1):
            wait_weights(g, layer)
        if g == 0:
            wait_start(0)
        widen(g, HALO, ROWS)
        tasks(g, OWN)

        wait_halo(1)

        @pl.when(t == 0)
        def _():
            ha[g, pl.ds(FAR, ROWS), :] = jnp.zeros((ROWS, C), jnp.bfloat16)

        widen(g, FAR, ROWS)
        tasks(g, NEAR)
        for cp in b_copies[g][0]:
            cp.start()
        wait_weights(g, 4)

        wait_halo(2)

        @pl.when(t < 2)
        def _():
            ha[g, pl.ds(0, FAR), :] = jnp.zeros((FAR, C), jnp.bfloat16)

        widen(g, 0, FAR)
        tasks(g, DISTANT)
        for cp in b_copies[g][1]:
            cp.start()
        if g == 0:
            @pl.when(x > 0)
            def _():
                skip_hand.wait_recv()
                sk[...] += skin[...].astype(jnp.float32)
        last_layer(g, 0)
        last_layer(g, 1)
        if g == 0:
            @pl.when(x == 3)
            def _():
                send_out(0)

    @pl.when(x < 3)
    def _():
        for cp in hand:
            cp.wait_send()
        skip_hand.start()
        skip_hand.wait_send()
        pl.semaphore_signal(done, inc=1, device_id=(x * 2 + other, tm), device_id_type=MESH)
        pl.semaphore_wait(done, 1)
        send_out(0)

    send_out(1)
    for m in range(2):
        pltpu.make_async_copy(made.at[0], result.at[m], o_sem.at[m]).wait()

    quarter.wait_send()

    @pl.when(x > 0)
    def _():
        first_rows(0, 0, QUARTER, first).wait_send()

    first_rows(1, 0, QUARTER, first).wait_send()

    @pl.when(x == 1)
    def _():
        first_rows(2, 16, QUARTER - 16, QUARTER + 16).wait_send()

    @pl.when(x > 1)
    def _():
        first_rows(2, 0, QUARTER, first).wait_send()

    for g in range(2):
        @pl.when(away[g])
        def _():
            outs[g][0].wait_send()

    for cp in w_copies:
        cp.wait_send()
    for cp in inner[2:]:
        cp.wait_send()
    for g in range(2):
        for cp in b_copies[g][0] + b_copies[g][1]:
            cp.wait_send()


def shards(signal, conv_weight, conv_bias, out_weight, out_bias):
    bf16, f32 = jnp.bfloat16, jnp.float32
    any_space = pl.BlockSpec(memory_space=pl.ANY)
    vmem = pl.BlockSpec(memory_space=pltpu.VMEM)
    dma = pltpu.SemaphoreType.DMA
    result = pl.pallas_call(
        kernel,
        out_shape=jax.ShapeDtypeStruct((2, 2, ROWS, C), bf16),
        in_specs=[any_space] * 5,
        out_specs=vmem,
        scratch_shapes=[
            pltpu.VMEM((2, LAYERS, 3 * C, 2 * C), bf16),
            pltpu.VMEM((2, LAYERS, C, 2 * C), bf16),
            pltpu.VMEM((2, LAYERS, 1, 2 * C), f32),
            pltpu.VMEM((2, LAYERS, 1, 2 * C), f32),
            pltpu.VMEM((2, SPAN, C), bf16),
            pltpu.VMEM((SPAN, C), f32),
            pltpu.VMEM((SPAN, C), f32),
            pltpu.VMEM((3, SPAN, C), bf16),
            pltpu.VMEM((2, ROWS, C), bf16),
            pltpu.VMEM((2, 2, ROWS, C), bf16),
            pltpu.VMEM((ROWS, C), bf16),
            pltpu.VMEM((ROWS, C), f32),
            pltpu.VMEM((ROWS, C), bf16),
            pltpu.VMEM((2, 2, ROWS, C), bf16),
            pltpu.VMEM((QUARTER, C), bf16),
            dma((12,)), dma((2, 12)),
            dma((3, 2)), dma((2, 3, 2)),
            dma, dma, dma((3,)),
            dma((2, 2, 2)), dma((2, 2, 2)),
            dma((3, 2)), dma, dma,
            dma((2,)), dma((2,)), pltpu.SemaphoreType.REGULAR,
        ],
        compiler_params=pltpu.CompilerParams(
            collective_id=0, has_side_effects=True, vmem_limit_bytes=63 * 1024 * 1024),
        cost_estimate=pl.CostEstimate(flops=2 * 2336 * 262144, bytes_accessed=4_000_000, transcendentals=2 * 2336 * 256),
    )(signal, conv_weight, conv_bias.reshape(LAYERS, 1, 2 * C), out_weight, out_bias.reshape(LAYERS, 1, 2 * C))
    return result[None, :, 0], result[None, :, 1].astype(f32)


def solution(mesh):
    return jax.shard_map(
        shards,
        mesh=mesh,
        in_specs=(
            P(None, "tm", None),
            P("section", None, None, None),
            P("section", None, None),
            P("section", None, None, None),
            P("section", None, None),
        ),
        out_specs=(P("section", None, "tm", None), P("section", None, "tm", None)),
        check_vma=False,
    )
```

```python
import jax
import jax.numpy as jnp
from jax import lax
from jax.experimental import pallas as pl
from jax.experimental.pallas import tpu as pltpu
from jax.sharding import PartitionSpec as P

MESH = pl.DeviceIdType.MESH
C = 128
ROWS = 256
NB = 64
FAR = 176
HALO = FAR + ROWS
SPAN = HALO + ROWS
LAYERS = 5
SPANS = (1, 16, 64, 128, 512)
QUARTER = 64
CUT = 176
EARLY = (CUT, ROWS)
LATE = (0, CUT)
OWN = ((0, 16, ROWS), (1, 48, ROWS), (2, 176, ROWS))
NEAR = ((0, -240, 16), (1, -208, 48), (2, -80, 176), (3, 176, ROWS))
DISTANT = ((0, -416, -240), (1, -384, -208), (2, -256, -80), (3, 0, 176))


def kernel(signal, conv_w, conv_b, out_w, out_b, result,
           wc, wo, bc, bo, ha, h0f, hbuf, xb, xo, xback, hend, sk, skin, made, relay,
           wsend, wsem, a_send, a_sem, r_send, r_sem, init_send, b_send, b_sem, h_send, s_send, s_sem,
           o_send, o_sem, done, taken):
    section = lax.axis_index("section")
    tm = lax.axis_index("tm")
    x, c = section // 2, section % 2
    y, z = tm // 16, tm % 16
    turned = (y + 3 + c) % 4
    pos = z * 4 + (turned ^ (turned >> 1))
    t = jnp.where(c == 1, pos, NB - 1 - pos)
    step = 2 * c - 1

    def tm_of(p, rec):
        n = p % 4
        return (((n ^ (n >> 1)) + 1 - rec) % 4) * 16 + p // 4

    def ahead(k):
        return tm_of((pos + step * k + NB) % NB, c)

    def worker(block, rec):
        return tm_of(jnp.where(rec == 1, block, NB - 1 - block), rec)

    other = 1 - c
    mine = jnp.where(tm == t, 1, 0)

    barrier = pltpu.get_barrier_semaphore()

    def greet(sec, where):
        pl.semaphore_signal(barrier, inc=1, device_id=(sec, where), device_id_type=MESH)

    greet(x * 2 + other, tm)
    for k in (1, 2, 4):
        greet(section, ahead(-k))

    @pl.when(x > 0)
    def _():
        for k in range(3):
            greet(section - 2, ahead(-k))

    greet(x * 2 + other, t)

    @pl.when(x == 0)
    def _():
        for plane in range(4):
            for k in range(3):
                if plane > 0 or k == 1:
                    greet(plane * 2 + c, ahead(-k))

    for m in range(2):
        @pl.when(jnp.logical_or(c != m, tm != worker(tm, m)))
        def _():
            greet(x * 2 + m, worker(tm, m))

    pl.semaphore_wait(barrier, 7 - mine + jnp.where(x < 3, 3, 0) + jnp.where(x == 0, 1, 3))

    def remote(src, dst, send, recv, sec, where):
        return pltpu.make_async_remote_copy(
            src_ref=src, dst_ref=dst, send_sem=send, recv_sem=recv,
            device_id=(sec, where), device_id_type=MESH)

    quarter = remote(signal.at[other, pl.ds(pl.multiple_of(x * QUARTER, QUARTER), QUARTER)], relay, r_send, r_sem,
                     x * 2 + other, worker(tm, other))
    quarter.start()

    parts = (
        ((EARLY, HALO), (LATE, HALO)),
        ((EARLY, FAR), (LATE, FAR)),
        ((EARLY, FAR - ROWS), ((ROWS - FAR, CUT), FAR - ROWS)),
    )

    def start_copies(g, src, sends, sec):
        out = []
        for k in range(3):
            for i, ((lo, hi), base) in enumerate(parts[k]):
                out.append(remote(src.at[pl.ds(lo, hi - lo)], ha.at[g, pl.ds(base + lo, hi - lo)],
                                  sends.at[k, i], a_sem.at[g, k, i if g else 0], sec, ahead(k)))
        return out

    jobs = []
    for layer in range(LAYERS):
        jobs.append((conv_w.at[0, layer], lambda g, l=layer: wc.at[g, l]))
        jobs.append((out_w.at[0, layer], lambda g, l=layer: wo.at[g, l]))
        if layer == 0:
            jobs.append((conv_b, lambda g: bc.at[g]))
            jobs.append((out_b, lambda g: bo.at[g]))
    w_copies = []
    for i, (src, dst) in enumerate(jobs):
        cp = remote(src, dst(c), wsend.at[i], wsem.at[c, i], x * 2 + other, tm)
        cp.start()
        w_copies.append(cp)
        pltpu.make_async_copy(src, dst(c), wsem.at[c, i]).start()
    need = {0: (0, 1, 2, 3), 1: (4, 5), 2: (6, 7), 3: (8, 9), 4: (10, 11)}

    def wait_weights(g, layer):
        for i in need[layer]:
            src, dst = jobs[i]
            pltpu.make_async_copy(src, dst(g), wsem.at[g, i]).wait()

    def dense(taps, g, layer, own):
        pre = jnp.dot(jnp.concatenate(taps, axis=1), wc[g, layer],
                      preferred_element_type=jnp.float32) + bc[g, layer]
        pre = pre.astype(jnp.bfloat16)
        half = jnp.bfloat16(0.5)
        gated = jnp.tanh(pre[:, :C]) * (half * jnp.tanh(half * pre[:, C:]) + half)
        if own:
            return jnp.dot(gated, wo[g, layer], preferred_element_type=jnp.float32) + bo[g, layer]
        return (jnp.dot(gated, wo[g, layer, :, pl.ds(0, C)], preferred_element_type=jnp.float32)
                + bo[g, layer, :, pl.ds(0, C)])

    next_section = jnp.where(x < 3, section + 2, section - 6)
    hand = start_copies(0, hend, h_send, next_section)
    skip_hand = remote(made.at[1, 1], skin, s_send, s_sem, next_section, ahead(0))
    inner = start_copies(1, ha.at[1, pl.ds(HALO, ROWS)], a_send, section)
    b_copies = [[[remote(xo.at[g, pl.ds(lo, hi - lo)], xback.at[g, i, pl.ds(lo, hi - lo)],
                         b_send.at[g, i, j], b_sem.at[g, i, j], section, ahead(k))
                  for i, k in enumerate((2, 4))]
                 for j, (lo, hi) in enumerate((EARLY, LATE))] for g in range(2)]
    away = [jnp.logical_or(c != g, mine == 0) for g in range(2)]
    outs = [(remote(made.at[g], result.at[c], o_send.at[g], o_sem.at[c], x * 2 + g, t),
             pltpu.make_async_copy(made.at[g], result.at[c], o_sem.at[c])) for g in range(2)]

    def send_out(g):
        far, near = outs[g]

        @pl.when(away[g])
        def _():
            far.start()

        @pl.when(jnp.logical_not(away[g]))
        def _():
            near.start()

    def first_rows(k, row, n, start):
        base = (HALO, FAR, FAR - ROWS)[k]
        return remote(relay.at[pl.ds(row, n)], ha.at[0, pl.ds(pl.multiple_of(base + start, 16), n)],
                      init_send.at[k], a_sem.at[0, k, 0], c, ahead(k))

    first = x * QUARTER
    quarter.wait_recv()

    @pl.when(x == 0)
    def _():
        pltpu.make_async_copy(relay, ha.at[0, pl.ds(HALO, QUARTER)], a_sem.at[0, 0, 0]).start()
        first_rows(1, 0, QUARTER, 0).start()

    @pl.when(x > 0)
    def _():
        first_rows(0, 0, QUARTER, first).start()
        first_rows(1, 0, QUARTER, first).start()

    @pl.when(x == 1)
    def _():
        first_rows(2, 16, QUARTER - 16, QUARTER + 16).start()

    @pl.when(x > 1)
    def _():
        first_rows(2, 0, QUARTER, first).start()

    def wait_start(k):
        rows = (pl.ds(HALO, ROWS), pl.ds(FAR, ROWS), pl.ds(0, FAR))[k]
        pltpu.make_async_copy(ha.at[0, rows], ha.at[0, rows], a_sem.at[0, k, 0]).wait()

    seen1 = jnp.where(t >= 1, 1.0, 0.0).astype(jnp.float32)
    seen2 = jnp.where(t >= 2, 1.0, 0.0).astype(jnp.float32)

    def tasks(g, todo):
        for layer, first, last in todo:
            d = SPANS[layer]
            for lo, hi in ((first, last),):
                at, n = lo + HALO, hi - lo
                if layer == 0:
                    taps = [h0f[pl.ds(at - 2, n), :].astype(jnp.bfloat16),
                            h0f[pl.ds(at - 1, n), :].astype(jnp.bfloat16),
                            ha[g, pl.ds(at, n), :]]
                    before = h0f
                else:
                    src = xb.at[layer - 1]
                    taps = [src[pl.ds(at - 2 * d, n), :], src[pl.ds(at - d, n), :], src[pl.ds(at, n), :]]
                    before = hbuf
                post = dense(taps, g, layer, hi > 0)
                h = before[pl.ds(at, n), :] + post[:, :C]
                hbuf[pl.ds(at, n), :] = h
                for begin, end, seen in ((-HALO, -ROWS, seen2), (-ROWS, 0, seen1), (0, ROWS, None)):
                    i, j = max(begin, lo), min(end, hi)
                    if i >= j:
                        continue
                    part = h[i - lo:j - lo]
                    if seen is not None:
                        part = part * seen
                    else:
                        s = post[i - lo:j - lo, C:]
                        if layer > 0 or g > 0:
                            s = s + sk[pl.ds(i, j - i), :]
                        sk[pl.ds(i, j - i), :] = s
                    if layer < 3:
                        xb[layer, pl.ds(i + HALO, j - i), :] = part.astype(jnp.bfloat16)
                    else:
                        xo[g, pl.ds(i, j - i), :] = part.astype(jnp.bfloat16)

    def last_layer(g, j):
        lo, hi = (EARLY, LATE)[j]
        rows = pl.ds(lo, hi - lo)
        for cp in b_copies[g][j]:
            cp.wait_recv()

        @pl.when(t < 4)
        def _():
            xback[g, 1, rows] = jnp.zeros((hi - lo, C), jnp.bfloat16)

        @pl.when(t < 2)
        def _():
            xback[g, 0, rows] = jnp.zeros((hi - lo, C), jnp.bfloat16)

        post = dense([xback[g, 1, rows, :], xback[g, 0, rows, :], xo[g, rows, :]], g, 4, True)
        h = (hbuf[pl.ds(lo + HALO, hi - lo), :] + post[:, :C]).astype(jnp.bfloat16)
        if g == 0:
            ha[1, pl.ds(HALO + lo, hi - lo), :] = h
            for k in (1, 2):
                inner[2 * k + j].start()
        else:
            hend[rows, :] = h

            @pl.when(x < 3)
            def _():
                for k in range(3):
                    hand[2 * k + j].start()
        skip = sk[rows, :] + post[:, C:]
        sk[rows, :] = skip
        made[g, 0, rows, :] = h
        made[g, 1, rows, :] = skip.astype(jnp.bfloat16)

    def widen(g, lo, n):
        h0f[pl.ds(lo, n), :] = ha[g, pl.ds(lo, n), :].astype(jnp.float32)

    for g in range(2):
        def wait_halo(k):
            if g == 0:
                wait_start(k)
            else:
                for cp in inner[2 * k:2 * k + 2]:
                    cp.wait_recv()

        for layer in range(LAYERS - 1):
            wait_weights(g, layer)
        if g == 0:
            wait_start(0)
        widen(g, HALO, ROWS)
        tasks(g, OWN)

        wait_halo(1)

        @pl.when(t == 0)
        def _():
            ha[g, pl.ds(FAR, ROWS), :] = jnp.zeros((ROWS, C), jnp.bfloat16)

        widen(g, FAR, ROWS)
        tasks(g, NEAR)
        for cp in b_copies[g][0]:
            cp.start()
        wait_weights(g, 4)

        wait_halo(2)
        if g == 0:
            @pl.when(x > 0)
            def _():
                pl.semaphore_signal(taken, inc=1, device_id=(section - 2, tm), device_id_type=MESH)

        @pl.when(t < 2)
        def _():
            ha[g, pl.ds(0, FAR), :] = jnp.zeros((FAR, C), jnp.bfloat16)

        widen(g, 0, FAR)
        tasks(g, DISTANT)
        for cp in b_copies[g][1]:
            cp.start()
        if g == 0:
            @pl.when(x > 0)
            def _():
                skip_hand.wait_recv()
                sk[...] += skin[...].astype(jnp.float32)
        last_layer(g, 0)
        last_layer(g, 1)
        if g == 0:
            @pl.when(x == 3)
            def _():
                send_out(0)

    @pl.when(x < 3)
    def _():
        for cp in hand:
            cp.wait_send()
        skip_hand.start()
        skip_hand.wait_send()
        pl.semaphore_wait(taken, 1)
        pl.semaphore_signal(done, inc=1, device_id=(x * 2 + other, tm), device_id_type=MESH)
        pl.semaphore_wait(done, 1)
        send_out(0)

    send_out(1)
    for m in range(2):
        pltpu.make_async_copy(made.at[0], result.at[m], o_sem.at[m]).wait()

    quarter.wait_send()

    @pl.when(x > 0)
    def _():
        first_rows(0, 0, QUARTER, first).wait_send()

    first_rows(1, 0, QUARTER, first).wait_send()

    @pl.when(x == 1)
    def _():
        first_rows(2, 16, QUARTER - 16, QUARTER + 16).wait_send()

    @pl.when(x > 1)
    def _():
        first_rows(2, 0, QUARTER, first).wait_send()

    for g in range(2):
        @pl.when(away[g])
        def _():
            outs[g][0].wait_send()

    for cp in w_copies:
        cp.wait_send()
    for cp in inner[2:]:
        cp.wait_send()
    for g in range(2):
        for cp in b_copies[g][0] + b_copies[g][1]:
            cp.wait_send()


def shards(signal, conv_weight, conv_bias, out_weight, out_bias):
    bf16, f32 = jnp.bfloat16, jnp.float32
    any_space = pl.BlockSpec(memory_space=pl.ANY)
    vmem = pl.BlockSpec(memory_space=pltpu.VMEM)
    dma = pltpu.SemaphoreType.DMA
    result = pl.pallas_call(
        kernel,
        out_shape=jax.ShapeDtypeStruct((2, 2, ROWS, C), bf16),
        in_specs=[any_space] * 5,
        out_specs=vmem,
        scratch_shapes=[
            pltpu.VMEM((2, LAYERS, 3 * C, 2 * C), bf16),
            pltpu.VMEM((2, LAYERS, C, 2 * C), bf16),
            pltpu.VMEM((2, LAYERS, 1, 2 * C), f32),
            pltpu.VMEM((2, LAYERS, 1, 2 * C), f32),
            pltpu.VMEM((2, SPAN, C), bf16),
            pltpu.VMEM((SPAN, C), f32),
            pltpu.VMEM((SPAN, C), f32),
            pltpu.VMEM((3, SPAN, C), bf16),
            pltpu.VMEM((2, ROWS, C), bf16),
            pltpu.VMEM((2, 2, ROWS, C), bf16),
            pltpu.VMEM((ROWS, C), bf16),
            pltpu.VMEM((ROWS, C), f32),
            pltpu.VMEM((ROWS, C), bf16),
            pltpu.VMEM((2, 2, ROWS, C), bf16),
            pltpu.VMEM((QUARTER, C), bf16),
            dma((12,)), dma((2, 12)),
            dma((3, 2)), dma((2, 3, 2)),
            dma, dma, dma((3,)),
            dma((2, 2, 2)), dma((2, 2, 2)),
            dma((3, 2)), dma, dma,
            dma((2,)), dma((2,)),
            pltpu.SemaphoreType.REGULAR, pltpu.SemaphoreType.REGULAR,
        ],
        compiler_params=pltpu.CompilerParams(
            collective_id=0, has_side_effects=True, vmem_limit_bytes=63 * 1024 * 1024),
        cost_estimate=pl.CostEstimate(flops=2 * 2336 * 262144, bytes_accessed=4_000_000, transcendentals=2 * 2336 * 256),
    )(signal, conv_weight, conv_bias.reshape(LAYERS, 1, 2 * C), out_weight, out_bias.reshape(LAYERS, 1, 2 * C))
    return result[None, :, 0], result[None, :, 1].astype(f32)


def solution(mesh):
    return jax.shard_map(
        shards,
        mesh=mesh,
        in_specs=(
            P(None, "tm", None),
            P("section", None, None, None),
            P("section", None, None),
            P("section", None, None, None),
            P("section", None, None),
        ),
        out_specs=(P("section", None, "tm", None), P("section", None, "tm", None)),
        check_vma=False,
    )
```

```python
import jax
import jax.numpy as jnp
from jax import lax
from jax.experimental import pallas as pl
from jax.experimental.pallas import tpu as pltpu
from jax.sharding import PartitionSpec as P

MESH = pl.DeviceIdType.MESH
C = 128
ROWS = 256
NB = 64
FAR = 176
HALO = FAR + ROWS
SPAN = HALO + ROWS
LAYERS = 5
SPANS = (1, 16, 64, 128, 512)
QUARTER = 64
CHUNK = 256
OWN = ((0, 16, ROWS), (1, 48, ROWS), (2, 176, ROWS))
AFTER = ((0, -416, 16), (1, -384, 48), (2, -256, 176), (3, 0, ROWS))


def pieces(lo, hi):
    count = -(-(hi - lo) // CHUNK)
    size = -(-(hi - lo) // (16 * count)) * 16
    return [(at, min(at + size, hi)) for at in range(lo, hi, size)]


def kernel(signal, conv_w, conv_b, out_w, out_b, result,
           wc, wo, bc, bo, ha, h0f, hbuf, xb, xo, xback, hend, sk, skin, made, relay,
           wsend, wsem, a_send, a_sem, r_send, r_sem, init_send, b_send, b_sem, h_send, s_send, s_sem,
           o_send, o_sem, done, taken):
    section = lax.axis_index("section")
    tm = lax.axis_index("tm")
    x, c = section // 2, section % 2
    y, z = tm // 16, tm % 16
    turned = (y + 3 + c) % 4
    pos = z * 4 + (turned ^ (turned >> 1))
    t = jnp.where(c == 1, pos, NB - 1 - pos)
    step = 2 * c - 1

    def tm_of(p, rec):
        n = p % 4
        return (((n ^ (n >> 1)) + 1 - rec) % 4) * 16 + p // 4

    def ahead(k):
        return tm_of((pos + step * k + NB) % NB, c)

    def worker(block, rec):
        return tm_of(jnp.where(rec == 1, block, NB - 1 - block), rec)

    other = 1 - c
    mine = jnp.where(tm == t, 1, 0)

    barrier = pltpu.get_barrier_semaphore()

    def greet(sec, where):
        pl.semaphore_signal(barrier, inc=1, device_id=(sec, where), device_id_type=MESH)

    greet(x * 2 + other, tm)
    for k in (1, 2, 4):
        greet(section, ahead(-k))

    @pl.when(x > 0)
    def _():
        for k in range(3):
            greet(section - 2, ahead(-k))

    greet(x * 2 + other, t)

    @pl.when(x == 0)
    def _():
        for plane in range(4):
            for k in range(3):
                if plane > 0 or k == 1:
                    greet(plane * 2 + c, ahead(-k))

    for m in range(2):
        @pl.when(jnp.logical_or(c != m, tm != worker(tm, m)))
        def _():
            greet(x * 2 + m, worker(tm, m))

    pl.semaphore_wait(barrier, 7 - mine + jnp.where(x < 3, 3, 0) + jnp.where(x == 0, 1, 3))

    def remote(src, dst, send, recv, sec, where):
        return pltpu.make_async_remote_copy(
            src_ref=src, dst_ref=dst, send_sem=send, recv_sem=recv,
            device_id=(sec, where), device_id_type=MESH)

    quarter = remote(signal.at[other, pl.ds(pl.multiple_of(x * QUARTER, QUARTER), QUARTER)], relay, r_send, r_sem,
                     x * 2 + other, worker(tm, other))
    quarter.start()

    parts = ((0, ROWS, HALO), (0, ROWS, FAR), (ROWS - FAR, FAR, 0))

    def start_copies(g, src, sends, sec):
        return [remote(src.at[pl.ds(lo, n)], ha.at[g, pl.ds(at, n)], sends.at[k], a_sem.at[g, k], sec, ahead(k))
                for k, (lo, n, at) in enumerate(parts)]

    jobs = []
    for layer in range(LAYERS):
        jobs.append((conv_w.at[0, layer], lambda g, l=layer: wc.at[g, l]))
        jobs.append((out_w.at[0, layer], lambda g, l=layer: wo.at[g, l]))
        if layer == 0:
            jobs.append((conv_b, lambda g: bc.at[g]))
            jobs.append((out_b, lambda g: bo.at[g]))
    w_copies = []
    for i, (src, dst) in enumerate(jobs):
        cp = remote(src, dst(c), wsend.at[i], wsem.at[c, i], x * 2 + other, tm)
        cp.start()
        w_copies.append(cp)
        pltpu.make_async_copy(src, dst(c), wsem.at[c, i]).start()
    need = {0: (0, 1, 2, 3), 1: (4, 5), 2: (6, 7), 3: (8, 9), 4: (10, 11)}

    def wait_weights(g, layer):
        for i in need[layer]:
            src, dst = jobs[i]
            pltpu.make_async_copy(src, dst(g), wsem.at[g, i]).wait()

    def dense(taps, g, layer, own):
        pre = jnp.dot(jnp.concatenate(taps, axis=1), wc[g, layer],
                      preferred_element_type=jnp.float32) + bc[g, layer]
        pre = pre.astype(jnp.bfloat16)
        half = jnp.bfloat16(0.5)
        gated = jnp.tanh(pre[:, :C]) * (half * jnp.tanh(half * pre[:, C:]) + half)
        if own:
            return jnp.dot(gated, wo[g, layer], preferred_element_type=jnp.float32) + bo[g, layer]
        return (jnp.dot(gated, wo[g, layer, :, pl.ds(0, C)], preferred_element_type=jnp.float32)
                + bo[g, layer, :, pl.ds(0, C)])

    next_section = jnp.where(x < 3, section + 2, section - 6)
    hand = start_copies(0, hend, h_send, next_section)
    skip_hand = remote(made.at[1, 1], skin, s_send, s_sem, next_section, ahead(0))
    inner = start_copies(1, ha.at[1, pl.ds(HALO, ROWS)], a_send, section)
    b_copies = [[remote(xo.at[g], xback.at[g, i], b_send.at[g, i], b_sem.at[g, i], section, ahead(k))
                 for i, k in enumerate((2, 4))] for g in range(2)]
    away = [jnp.logical_or(c != g, mine == 0) for g in range(2)]
    outs = [(remote(made.at[g], result.at[c], o_send.at[g], o_sem.at[c], x * 2 + g, t),
             pltpu.make_async_copy(made.at[g], result.at[c], o_sem.at[c])) for g in range(2)]

    def send_out(g):
        far, near = outs[g]

        @pl.when(away[g])
        def _():
            far.start()

        @pl.when(jnp.logical_not(away[g]))
        def _():
            near.start()

    def first_rows(k, row, n, start):
        base = (HALO, FAR, FAR - ROWS)[k]
        return remote(relay.at[pl.ds(row, n)], ha.at[0, pl.ds(pl.multiple_of(base + start, 16), n)],
                      init_send.at[k], a_sem.at[0, k], c, ahead(k))

    first = x * QUARTER
    quarter.wait_recv()

    @pl.when(x == 0)
    def _():
        pltpu.make_async_copy(relay, ha.at[0, pl.ds(HALO, QUARTER)], a_sem.at[0, 0]).start()
        first_rows(1, 0, QUARTER, 0).start()

    @pl.when(x > 0)
    def _():
        first_rows(0, 0, QUARTER, first).start()
        first_rows(1, 0, QUARTER, first).start()

    @pl.when(x == 1)
    def _():
        first_rows(2, 16, QUARTER - 16, QUARTER + 16).start()

    @pl.when(x > 1)
    def _():
        first_rows(2, 0, QUARTER, first).start()

    def wait_start(k):
        rows = (pl.ds(HALO, ROWS), pl.ds(FAR, ROWS), pl.ds(0, FAR))[k]
        pltpu.make_async_copy(ha.at[0, rows], ha.at[0, rows], a_sem.at[0, k]).wait()

    seen1 = jnp.where(t >= 1, 1.0, 0.0).astype(jnp.float32)
    seen2 = jnp.where(t >= 2, 1.0, 0.0).astype(jnp.float32)

    def tasks(g, todo):
        for layer, first, last in todo:
            d = SPANS[layer]
            for lo, hi in pieces(first, last):
                at, n = lo + HALO, hi - lo
                if layer == 0:
                    taps = [h0f[pl.ds(at - 2, n), :].astype(jnp.bfloat16),
                            h0f[pl.ds(at - 1, n), :].astype(jnp.bfloat16),
                            ha[g, pl.ds(at, n), :]]
                    before = h0f
                else:
                    src = xb.at[layer - 1]
                    taps = [src[pl.ds(at - 2 * d, n), :], src[pl.ds(at - d, n), :], src[pl.ds(at, n), :]]
                    before = hbuf
                post = dense(taps, g, layer, hi > 0)
                h = before[pl.ds(at, n), :] + post[:, :C]
                hbuf[pl.ds(at, n), :] = h
                for begin, end, seen in ((-HALO, -ROWS, seen2), (-ROWS, 0, seen1), (0, ROWS, None)):
                    i, j = max(begin, lo), min(end, hi)
                    if i >= j:
                        continue
                    part = h[i - lo:j - lo]
                    if seen is not None:
                        part = part * seen
                    else:
                        s = post[i - lo:j - lo, C:]
                        if layer > 0 or g > 0:
                            s = s + sk[pl.ds(i, j - i), :]
                        sk[pl.ds(i, j - i), :] = s
                    if layer < 3:
                        xb[layer, pl.ds(i + HALO, j - i), :] = part.astype(jnp.bfloat16)
                    else:
                        xo[g, pl.ds(i, j - i), :] = part.astype(jnp.bfloat16)

    def last_layer(g):
        for cp in b_copies[g]:
            cp.wait_recv()

        @pl.when(t < 4)
        def _():
            xback[g, 1] = jnp.zeros((ROWS, C), jnp.bfloat16)

        @pl.when(t < 2)
        def _():
            xback[g, 0] = jnp.zeros((ROWS, C), jnp.bfloat16)

        for lo, hi in pieces(0, ROWS):
            rows = pl.ds(lo, hi - lo)
            post = dense([xback[g, 1, rows, :], xback[g, 0, rows, :], xo[g, rows, :]], g, 4, True)
            h = (hbuf[pl.ds(lo + HALO, hi - lo), :] + post[:, :C]).astype(jnp.bfloat16)
            if g == 0:
                ha[1, pl.ds(HALO + lo, hi - lo), :] = h
            else:
                hend[rows, :] = h
            skip = sk[rows, :] + post[:, C:]
            sk[rows, :] = skip
            made[g, 0, rows, :] = h
            made[g, 1, rows, :] = skip.astype(jnp.bfloat16)
        if g == 0:
            for cp in inner[1:]:
                cp.start()
        else:
            @pl.when(x < 3)
            def _():
                for cp in hand:
                    cp.start()

    def widen(g, lo, n):
        h0f[pl.ds(lo, n), :] = ha[g, pl.ds(lo, n), :].astype(jnp.float32)

    for g in range(2):
        def wait_halo(k):
            if g == 0:
                wait_start(k)
            else:
                inner[k].wait_recv()

        for layer in range(LAYERS - 1):
            wait_weights(g, layer)
        if g == 0:
            wait_start(0)
        widen(g, HALO, ROWS)
        tasks(g, OWN)

        wait_halo(1)
        wait_halo(2)
        if g == 0:
            @pl.when(x > 0)
            def _():
                pl.semaphore_signal(taken, inc=1, device_id=(section - 2, tm), device_id_type=MESH)

        @pl.when(t == 0)
        def _():
            ha[g, pl.ds(0, HALO), :] = jnp.zeros((HALO, C), jnp.bfloat16)

        @pl.when(t == 1)
        def _():
            ha[g, pl.ds(0, FAR), :] = jnp.zeros((FAR, C), jnp.bfloat16)

        widen(g, 0, HALO)
        tasks(g, AFTER)
        for cp in b_copies[g]:
            cp.start()
        wait_weights(g, 4)
        if g == 0:
            @pl.when(x > 0)
            def _():
                skip_hand.wait_recv()
                sk[...] += skin[...].astype(jnp.float32)
        last_layer(g)
        if g == 0:
            @pl.when(x == 3)
            def _():
                send_out(0)

    @pl.when(x < 3)
    def _():
        for cp in hand:
            cp.wait_send()
        skip_hand.start()
        skip_hand.wait_send()
        pl.semaphore_wait(taken, 1)
        pl.semaphore_signal(done, inc=1, device_id=(x * 2 + other, tm), device_id_type=MESH)
        pl.semaphore_wait(done, 1)
        send_out(0)

    send_out(1)
    for m in range(2):
        pltpu.make_async_copy(made.at[0], result.at[m], o_sem.at[m]).wait()

    quarter.wait_send()

    @pl.when(x > 0)
    def _():
        first_rows(0, 0, QUARTER, first).wait_send()

    first_rows(1, 0, QUARTER, first).wait_send()

    @pl.when(x == 1)
    def _():
        first_rows(2, 16, QUARTER - 16, QUARTER + 16).wait_send()

    @pl.when(x > 1)
    def _():
        first_rows(2, 0, QUARTER, first).wait_send()

    for g in range(2):
        @pl.when(away[g])
        def _():
            outs[g][0].wait_send()

    for cp in w_copies:
        cp.wait_send()
    for cp in inner[1:]:
        cp.wait_send()
    for g in range(2):
        for cp in b_copies[g]:
            cp.wait_send()


def shards(signal, conv_weight, conv_bias, out_weight, out_bias):
    bf16, f32 = jnp.bfloat16, jnp.float32
    any_space = pl.BlockSpec(memory_space=pl.ANY)
    vmem = pl.BlockSpec(memory_space=pltpu.VMEM)
    dma = pltpu.SemaphoreType.DMA
    result = pl.pallas_call(
        kernel,
        out_shape=jax.ShapeDtypeStruct((2, 2, ROWS, C), bf16),
        in_specs=[any_space] * 5,
        out_specs=vmem,
        scratch_shapes=[
            pltpu.VMEM((2, LAYERS, 3 * C, 2 * C), bf16),
            pltpu.VMEM((2, LAYERS, C, 2 * C), bf16),
            pltpu.VMEM((2, LAYERS, 1, 2 * C), f32),
            pltpu.VMEM((2, LAYERS, 1, 2 * C), f32),
            pltpu.VMEM((2, SPAN, C), bf16),
            pltpu.VMEM((SPAN, C), f32),
            pltpu.VMEM((SPAN, C), f32),
            pltpu.VMEM((3, SPAN, C), bf16),
            pltpu.VMEM((2, ROWS, C), bf16),
            pltpu.VMEM((2, 2, ROWS, C), bf16),
            pltpu.VMEM((ROWS, C), bf16),
            pltpu.VMEM((ROWS, C), f32),
            pltpu.VMEM((ROWS, C), bf16),
            pltpu.VMEM((2, 2, ROWS, C), bf16),
            pltpu.VMEM((QUARTER, C), bf16),
            dma((12,)), dma((2, 12)),
            dma((3,)), dma((2, 3)),
            dma, dma, dma((3,)),
            dma((2, 2)), dma((2, 2)),
            dma((3,)), dma, dma,
            dma((2,)), dma((2,)),
            pltpu.SemaphoreType.REGULAR, pltpu.SemaphoreType.REGULAR,
        ],
        compiler_params=pltpu.CompilerParams(
            collective_id=0, has_side_effects=True, vmem_limit_bytes=63 * 1024 * 1024),
        cost_estimate=pl.CostEstimate(flops=2 * 2336 * 262144, bytes_accessed=4_000_000, transcendentals=2 * 2336 * 256),
    )(signal, conv_weight, conv_bias.reshape(LAYERS, 1, 2 * C), out_weight, out_bias.reshape(LAYERS, 1, 2 * C))
    return result[None, :, 0], result[None, :, 1].astype(f32)


def solution(mesh):
    return jax.shard_map(
        shards,
        mesh=mesh,
        in_specs=(
            P(None, "tm", None),
            P("section", None, None, None),
            P("section", None, None),
            P("section", None, None, None),
            P("section", None, None),
        ),
        out_specs=(P("section", None, "tm", None), P("section", None, "tm", None)),
        check_vma=False,
    )
```

```python
import jax
import jax.numpy as jnp
from jax import lax
from jax.experimental import pallas as pl
from jax.experimental.pallas import tpu as pltpu
from jax.sharding import PartitionSpec as P

MESH = pl.DeviceIdType.MESH
C = 128
ROWS = 256
NB = 64
FAR = 176
HALO = FAR + ROWS
SPAN = HALO + ROWS
LAYERS = 5
SPANS = (1, 16, 64, 128, 512)
QUARTER = 64
CHUNK = 256
OWN = ((0, 16, ROWS), (1, 48, ROWS), (2, 176, ROWS))
AFTER = ((0, -416, 16), (1, -384, 48), (2, -256, 176), (3, 0, ROWS))


def pieces(lo, hi):
    count = -(-(hi - lo) // CHUNK)
    size = -(-(hi - lo) // (16 * count)) * 16
    return [(at, min(at + size, hi)) for at in range(lo, hi, size)]


def kernel(signal, conv_w, conv_b, out_w, out_b, result,
           wc, wo, bc, bo, ha, h0f, hbuf, xb, xo, xback, hend, sk, skin, made, relay,
           wsend, wsem, a_send, a_sem, r_send, r_sem, init_send, b_send, b_sem, h_send, s_send, s_sem,
           o_send, o_sem, done, taken):
    section = lax.axis_index("section")
    tm = lax.axis_index("tm")
    x, c = section // 2, section % 2
    y, z = tm // 16, tm % 16
    turned = (y + 4 - c) % 4
    pos = z * 4 + (turned ^ (turned >> 1))
    t = jnp.where(c == 0, pos, NB - 1 - pos)
    step = 1 - 2 * c

    def tm_of(p, rec):
        n = p % 4
        return (((n ^ (n >> 1)) + rec) % 4) * 16 + p // 4

    def ahead(k):
        return tm_of((pos + step * k + NB) % NB, c)

    def worker(block, rec):
        return tm_of(jnp.where(rec == 0, block, NB - 1 - block), rec)

    other = 1 - c
    mine = jnp.where(tm == t, 1, 0)

    barrier = pltpu.get_barrier_semaphore()

    def greet(sec, where):
        pl.semaphore_signal(barrier, inc=1, device_id=(sec, where), device_id_type=MESH)

    greet(x * 2 + other, tm)
    for k in (1, 2, 4):
        greet(section, ahead(-k))

    @pl.when(x > 0)
    def _():
        for k in range(3):
            greet(section - 2, ahead(-k))

    greet(x * 2 + other, t)

    @pl.when(x == 0)
    def _():
        for plane in range(4):
            for k in range(3):
                if plane > 0 or k == 1:
                    greet(plane * 2 + c, ahead(-k))

    for m in range(2):
        @pl.when(jnp.logical_or(c != m, tm != worker(tm, m)))
        def _():
            greet(x * 2 + m, worker(tm, m))

    pl.semaphore_wait(barrier, 7 - mine + jnp.where(x < 3, 3, 0) + jnp.where(x == 0, 1, 3))

    def remote(src, dst, send, recv, sec, where):
        return pltpu.make_async_remote_copy(
            src_ref=src, dst_ref=dst, send_sem=send, recv_sem=recv,
            device_id=(sec, where), device_id_type=MESH)

    quarter = remote(signal.at[other, pl.ds(pl.multiple_of(x * QUARTER, QUARTER), QUARTER)], relay, r_send, r_sem,
                     x * 2 + other, worker(tm, other))
    quarter.start()

    parts = ((0, ROWS, HALO), (0, ROWS, FAR), (ROWS - FAR, FAR, 0))

    def start_copies(g, src, sends, sec):
        return [remote(src.at[pl.ds(lo, n)], ha.at[g, pl.ds(at, n)], sends.at[k], a_sem.at[g, k], sec, ahead(k))
                for k, (lo, n, at) in enumerate(parts)]

    jobs = []
    for layer in range(LAYERS):
        jobs.append((conv_w.at[0, layer], lambda g, l=layer: wc.at[g, l]))
        jobs.append((out_w.at[0, layer], lambda g, l=layer: wo.at[g, l]))
        if layer == 0:
            jobs.append((conv_b, lambda g: bc.at[g]))
            jobs.append((out_b, lambda g: bo.at[g]))
    w_copies = []
    for i, (src, dst) in enumerate(jobs):
        cp = remote(src, dst(c), wsend.at[i], wsem.at[c, i], x * 2 + other, tm)
        cp.start()
        w_copies.append(cp)
        pltpu.make_async_copy(src, dst(c), wsem.at[c, i]).start()
    need = {0: (0, 1, 2, 3), 1: (4, 5), 2: (6, 7), 3: (8, 9), 4: (10, 11)}

    def wait_weights(g, layer):
        for i in need[layer]:
            src, dst = jobs[i]
            pltpu.make_async_copy(src, dst(g), wsem.at[g, i]).wait()

    def dense(taps, g, layer, own):
        pre = jnp.dot(jnp.concatenate(taps, axis=1), wc[g, layer],
                      preferred_element_type=jnp.float32) + bc[g, layer]
        pre = pre.astype(jnp.bfloat16)
        half = jnp.bfloat16(0.5)
        gated = jnp.tanh(pre[:, :C]) * (half * jnp.tanh(half * pre[:, C:]) + half)
        if own:
            return jnp.dot(gated, wo[g, layer], preferred_element_type=jnp.float32) + bo[g, layer]
        return (jnp.dot(gated, wo[g, layer, :, pl.ds(0, C)], preferred_element_type=jnp.float32)
                + bo[g, layer, :, pl.ds(0, C)])

    next_section = jnp.where(x < 3, section + 2, section - 6)
    hand = start_copies(0, hend, h_send, next_section)
    skip_hand = remote(made.at[1, 1], skin, s_send, s_sem, next_section, ahead(0))
    inner = start_copies(1, ha.at[1, pl.ds(HALO, ROWS)], a_send, section)
    b_copies = [[remote(xo.at[g], xback.at[g, i], b_send.at[g, i], b_sem.at[g, i], section, ahead(k))
                 for i, k in enumerate((2, 4))] for g in range(2)]
    away = [jnp.logical_or(c != g, mine == 0) for g in range(2)]
    outs = [(remote(made.at[g], result.at[c], o_send.at[g], o_sem.at[c], x * 2 + g, t),
             pltpu.make_async_copy(made.at[g], result.at[c], o_sem.at[c])) for g in range(2)]

    def send_out(g):
        far, near = outs[g]

        @pl.when(away[g])
        def _():
            far.start()

        @pl.when(jnp.logical_not(away[g]))
        def _():
            near.start()

    def first_rows(k, row, n, start):
        base = (HALO, FAR, FAR - ROWS)[k]
        return remote(relay.at[pl.ds(row, n)], ha.at[0, pl.ds(pl.multiple_of(base + start, 16), n)],
                      init_send.at[k], a_sem.at[0, k], c, ahead(k))

    first = x * QUARTER
    quarter.wait_recv()

    @pl.when(x == 0)
    def _():
        pltpu.make_async_copy(relay, ha.at[0, pl.ds(HALO, QUARTER)], a_sem.at[0, 0]).start()
        first_rows(1, 0, QUARTER, 0).start()

    @pl.when(x > 0)
    def _():
        first_rows(0, 0, QUARTER, first).start()
        first_rows(1, 0, QUARTER, first).start()

    @pl.when(x == 1)
    def _():
        first_rows(2, 16, QUARTER - 16, QUARTER + 16).start()

    @pl.when(x > 1)
    def _():
        first_rows(2, 0, QUARTER, first).start()

    def wait_start(k):
        rows = (pl.ds(HALO, ROWS), pl.ds(FAR, ROWS), pl.ds(0, FAR))[k]
        pltpu.make_async_copy(ha.at[0, rows], ha.at[0, rows], a_sem.at[0, k]).wait()

    seen1 = jnp.where(t >= 1, 1.0, 0.0).astype(jnp.float32)
    seen2 = jnp.where(t >= 2, 1.0, 0.0).astype(jnp.float32)

    def tasks(g, todo):
        for layer, first, last in todo:
            d = SPANS[layer]
            for lo, hi in pieces(first, last):
                at, n = lo + HALO, hi - lo
                if layer == 0:
                    taps = [h0f[pl.ds(at - 2, n), :].astype(jnp.bfloat16),
                            h0f[pl.ds(at - 1, n), :].astype(jnp.bfloat16),
                            ha[g, pl.ds(at, n), :]]
                    before = h0f
                else:
                    src = xb.at[layer - 1]
                    taps = [src[pl.ds(at - 2 * d, n), :], src[pl.ds(at - d, n), :], src[pl.ds(at, n), :]]
                    before = hbuf
                post = dense(taps, g, layer, hi > 0)
                h = before[pl.ds(at, n), :] + post[:, :C]
                hbuf[pl.ds(at, n), :] = h
                for begin, end, seen in ((-HALO, -ROWS, seen2), (-ROWS, 0, seen1), (0, ROWS, None)):
                    i, j = max(begin, lo), min(end, hi)
                    if i >= j:
                        continue
                    part = h[i - lo:j - lo]
                    if seen is not None:
                        part = part * seen
                    else:
                        s = post[i - lo:j - lo, C:]
                        if layer > 0 or g > 0:
                            s = s + sk[pl.ds(i, j - i), :]
                        sk[pl.ds(i, j - i), :] = s
                    if layer < 3:
                        xb[layer, pl.ds(i + HALO, j - i), :] = part.astype(jnp.bfloat16)
                    else:
                        xo[g, pl.ds(i, j - i), :] = part.astype(jnp.bfloat16)

    def last_layer(g):
        for cp in b_copies[g]:
            cp.wait_recv()

        @pl.when(t < 4)
        def _():
            xback[g, 1] = jnp.zeros((ROWS, C), jnp.bfloat16)

        @pl.when(t < 2)
        def _():
            xback[g, 0] = jnp.zeros((ROWS, C), jnp.bfloat16)

        for lo, hi in pieces(0, ROWS):
            rows = pl.ds(lo, hi - lo)
            post = dense([xback[g, 1, rows, :], xback[g, 0, rows, :], xo[g, rows, :]], g, 4, True)
            h = (hbuf[pl.ds(lo + HALO, hi - lo), :] + post[:, :C]).astype(jnp.bfloat16)
            if g == 0:
                ha[1, pl.ds(HALO + lo, hi - lo), :] = h
            else:
                hend[rows, :] = h
            skip = sk[rows, :] + post[:, C:]
            sk[rows, :] = skip
            made[g, 0, rows, :] = h
            made[g, 1, rows, :] = skip.astype(jnp.bfloat16)
        if g == 0:
            for cp in inner[1:]:
                cp.start()
        else:
            @pl.when(x < 3)
            def _():
                for cp in hand:
                    cp.start()

    def widen(g, lo, n):
        h0f[pl.ds(lo, n), :] = ha[g, pl.ds(lo, n), :].astype(jnp.float32)

    for g in range(2):
        def wait_halo(k):
            if g == 0:
                wait_start(k)
            else:
                inner[k].wait_recv()

        for layer in range(LAYERS - 1):
            wait_weights(g, layer)
        if g == 0:
            wait_start(0)
        widen(g, HALO, ROWS)
        tasks(g, OWN)

        wait_halo(1)
        wait_halo(2)
        if g == 0:
            @pl.when(x > 0)
            def _():
                pl.semaphore_signal(taken, inc=1, device_id=(section - 2, tm), device_id_type=MESH)

        @pl.when(t == 0)
        def _():
            ha[g, pl.ds(0, HALO), :] = jnp.zeros((HALO, C), jnp.bfloat16)

        @pl.when(t == 1)
        def _():
            ha[g, pl.ds(0, FAR), :] = jnp.zeros((FAR, C), jnp.bfloat16)

        widen(g, 0, HALO)
        tasks(g, AFTER)
        for cp in b_copies[g]:
            cp.start()
        wait_weights(g, 4)
        if g == 0:
            @pl.when(x > 0)
            def _():
                skip_hand.wait_recv()
                sk[...] += skin[...].astype(jnp.float32)
        last_layer(g)
        if g == 0:
            @pl.when(x == 3)
            def _():
                send_out(0)

    @pl.when(x < 3)
    def _():
        for cp in hand:
            cp.wait_send()
        skip_hand.start()
        skip_hand.wait_send()
        pl.semaphore_wait(taken, 1)
        pl.semaphore_signal(done, inc=1, device_id=(x * 2 + other, tm), device_id_type=MESH)
        pl.semaphore_wait(done, 1)
        send_out(0)

    send_out(1)
    for m in range(2):
        pltpu.make_async_copy(made.at[0], result.at[m], o_sem.at[m]).wait()

    quarter.wait_send()

    @pl.when(x > 0)
    def _():
        first_rows(0, 0, QUARTER, first).wait_send()

    first_rows(1, 0, QUARTER, first).wait_send()

    @pl.when(x == 1)
    def _():
        first_rows(2, 16, QUARTER - 16, QUARTER + 16).wait_send()

    @pl.when(x > 1)
    def _():
        first_rows(2, 0, QUARTER, first).wait_send()

    for g in range(2):
        @pl.when(away[g])
        def _():
            outs[g][0].wait_send()

    for cp in w_copies:
        cp.wait_send()
    for cp in inner[1:]:
        cp.wait_send()
    for g in range(2):
        for cp in b_copies[g]:
            cp.wait_send()


def shards(signal, conv_weight, conv_bias, out_weight, out_bias):
    bf16, f32 = jnp.bfloat16, jnp.float32
    any_space = pl.BlockSpec(memory_space=pl.ANY)
    vmem = pl.BlockSpec(memory_space=pltpu.VMEM)
    dma = pltpu.SemaphoreType.DMA
    result = pl.pallas_call(
        kernel,
        out_shape=jax.ShapeDtypeStruct((2, 2, ROWS, C), bf16),
        in_specs=[any_space] * 5,
        out_specs=vmem,
        scratch_shapes=[
            pltpu.VMEM((2, LAYERS, 3 * C, 2 * C), bf16),
            pltpu.VMEM((2, LAYERS, C, 2 * C), bf16),
            pltpu.VMEM((2, LAYERS, 1, 2 * C), f32),
            pltpu.VMEM((2, LAYERS, 1, 2 * C), f32),
            pltpu.VMEM((2, SPAN, C), bf16),
            pltpu.VMEM((SPAN, C), f32),
            pltpu.VMEM((SPAN, C), f32),
            pltpu.VMEM((3, SPAN, C), bf16),
            pltpu.VMEM((2, ROWS, C), bf16),
            pltpu.VMEM((2, 2, ROWS, C), bf16),
            pltpu.VMEM((ROWS, C), bf16),
            pltpu.VMEM((ROWS, C), f32),
            pltpu.VMEM((ROWS, C), bf16),
            pltpu.VMEM((2, 2, ROWS, C), bf16),
            pltpu.VMEM((QUARTER, C), bf16),
            dma((12,)), dma((2, 12)),
            dma((3,)), dma((2, 3)),
            dma, dma, dma((3,)),
            dma((2, 2)), dma((2, 2)),
            dma((3,)), dma, dma,
            dma((2,)), dma((2,)),
            pltpu.SemaphoreType.REGULAR, pltpu.SemaphoreType.REGULAR,
        ],
        compiler_params=pltpu.CompilerParams(
            collective_id=0, has_side_effects=True, vmem_limit_bytes=63 * 1024 * 1024),
        cost_estimate=pl.CostEstimate(flops=2 * 2336 * 262144, bytes_accessed=4_000_000, transcendentals=2 * 2336 * 256),
    )(signal, conv_weight, conv_bias.reshape(LAYERS, 1, 2 * C), out_weight, out_bias.reshape(LAYERS, 1, 2 * C))
    return result[None, :, 0], result[None, :, 1].astype(f32)


def solution(mesh):
    return jax.shard_map(
        shards,
        mesh=mesh,
        in_specs=(
            P(None, "tm", None),
            P("section", None, None, None),
            P("section", None, None),
            P("section", None, None, None),
            P("section", None, None),
        ),
        out_specs=(P("section", None, "tm", None), P("section", None, "tm", None)),
        check_vma=False,
    )
```

```python
import jax
import jax.numpy as jnp
from jax import lax
from jax.experimental import pallas as pl
from jax.experimental.pallas import tpu as pltpu
from jax.sharding import PartitionSpec as P

MESH = pl.DeviceIdType.MESH
C = 128
ROWS = 256
NB = 64
FAR = 176
HALO = FAR + ROWS
SPAN = HALO + ROWS
LAYERS = 5
SPANS = (1, 16, 64, 128, 512)
QUARTER = 64
CHUNK = 256
OWN = ((0, 16, ROWS), (1, 48, ROWS), (2, 176, ROWS))
AFTER = ((0, -416, 16), (1, -384, 48), (2, -256, 176), (3, 0, ROWS))


def pieces(lo, hi):
    count = -(-(hi - lo) // CHUNK)
    size = -(-(hi - lo) // (16 * count)) * 16
    return [(at, min(at + size, hi)) for at in range(lo, hi, size)]


def kernel(signal, conv_w, conv_b, out_w, out_b, result,
           wc, wo, bc, bo, ha, h0f, hbuf, xb, xo, xback, hend, sk, skin, made, relay, via,
           wsend, wsem, a_send, a_sem, r_send, r_sem, init_send, b_send, b_sem, h_send, s_send, s_sem,
           o_send, o_sem, v_send, v_sem, done, taken):
    section = lax.axis_index("section")
    tm = lax.axis_index("tm")
    x, c = section // 2, section % 2
    y, z = tm // 16, tm % 16
    turned = (y + 3 + c) % 4
    pos = z * 4 + (turned ^ (turned >> 1))
    t = jnp.where(c == 1, pos, NB - 1 - pos)
    step = 2 * c - 1

    def tm_of(p, rec):
        n = p % 4
        return (((n ^ (n >> 1)) + 1 - rec) % 4) * 16 + p // 4

    def ahead(k):
        return tm_of((pos + step * k + NB) % NB, c)

    def worker(block, rec):
        return tm_of(jnp.where(rec == 1, block, NB - 1 - block), rec)

    other = 1 - c
    mine = jnp.where(tm == t, 1, 0)

    barrier = pltpu.get_barrier_semaphore()

    def greet(sec, where):
        pl.semaphore_signal(barrier, inc=1, device_id=(sec, where), device_id_type=MESH)

    greet(x * 2 + other, tm)
    for k in (1, 2, 4):
        greet(section, ahead(-k))

    @pl.when(x > 0)
    def _():
        for k in range(3):
            greet(section - 2, ahead(-k))

    greet(x * 2 + other, t)

    @pl.when(x == 0)
    def _():
        for plane in range(4):
            for k in range(3):
                if plane > 0 or k == 1:
                    greet(plane * 2 + c, ahead(-k))

    by_way = jnp.logical_and(x == 3, c == 0)
    for m in range(2):
        @pl.when(jnp.logical_and(jnp.logical_not(by_way), jnp.logical_or(c != m, tm != worker(tm, m))))
        def _():
            greet(x * 2 + m, worker(tm, m))

        @pl.when(by_way)
        def _():
            greet(m, tm)

    @pl.when(x == 0)
    def _():
        greet(6 + c, worker(tm, c))

    pl.semaphore_wait(barrier, 7 - jnp.where(by_way, 0, mine) + jnp.where(x < 3, 3, 0) + jnp.where(x == 0, 2, 3))

    def remote(src, dst, send, recv, sec, where):
        return pltpu.make_async_remote_copy(
            src_ref=src, dst_ref=dst, send_sem=send, recv_sem=recv,
            device_id=(sec, where), device_id_type=MESH)

    quarter = remote(signal.at[other, pl.ds(pl.multiple_of(x * QUARTER, QUARTER), QUARTER)], relay, r_send, r_sem,
                     x * 2 + other, worker(tm, other))
    quarter.start()

    parts = ((0, ROWS, HALO), (0, ROWS, FAR), (ROWS - FAR, FAR, 0))

    def start_copies(g, src, sends, sec):
        return [remote(src.at[pl.ds(lo, n)], ha.at[g, pl.ds(at, n)], sends.at[k], a_sem.at[g, k], sec, ahead(k))
                for k, (lo, n, at) in enumerate(parts)]

    jobs = []
    for layer in range(LAYERS):
        jobs.append((conv_w.at[0, layer], lambda g, l=layer: wc.at[g, l]))
        jobs.append((out_w.at[0, layer], lambda g, l=layer: wo.at[g, l]))
        if layer == 0:
            jobs.append((conv_b, lambda g: bc.at[g]))
            jobs.append((out_b, lambda g: bo.at[g]))
    w_copies = []
    for i, (src, dst) in enumerate(jobs):
        cp = remote(src, dst(c), wsend.at[i], wsem.at[c, i], x * 2 + other, tm)
        cp.start()
        w_copies.append(cp)
        pltpu.make_async_copy(src, dst(c), wsem.at[c, i]).start()
    need = {0: (0, 1, 2, 3), 1: (4, 5), 2: (6, 7), 3: (8, 9), 4: (10, 11)}

    def wait_weights(g, layer):
        for i in need[layer]:
            src, dst = jobs[i]
            pltpu.make_async_copy(src, dst(g), wsem.at[g, i]).wait()

    def dense(taps, g, layer, own):
        pre = jnp.dot(jnp.concatenate(taps, axis=1), wc[g, layer],
                      preferred_element_type=jnp.float32) + bc[g, layer]
        pre = pre.astype(jnp.bfloat16)
        half = jnp.bfloat16(0.5)
        gated = jnp.tanh(pre[:, :C]) * (half * jnp.tanh(half * pre[:, C:]) + half)
        if own:
            return jnp.dot(gated, wo[g, layer], preferred_element_type=jnp.float32) + bo[g, layer]
        return (jnp.dot(gated, wo[g, layer, :, pl.ds(0, C)], preferred_element_type=jnp.float32)
                + bo[g, layer, :, pl.ds(0, C)])

    next_section = jnp.where(x < 3, section + 2, section - 6)
    hand = start_copies(0, hend, h_send, next_section)
    skip_hand = remote(made.at[1, 1], skin, s_send, s_sem, next_section, ahead(0))
    inner = start_copies(1, ha.at[1, pl.ds(HALO, ROWS)], a_send, section)
    b_copies = [[remote(xo.at[g], xback.at[g, i], b_send.at[g, i], b_sem.at[g, i], section, ahead(k))
                 for i, k in enumerate((2, 4))] for g in range(2)]
    away = [jnp.logical_or(c != g, mine == 0) for g in range(2)]
    outs = [(remote(made.at[g], result.at[c], o_send.at[g], o_sem.at[c], x * 2 + g, t),
             pltpu.make_async_copy(made.at[g], result.at[c], o_sem.at[c])) for g in range(2)]

    to_way = remote(made.at[0], via, o_send.at[0], v_sem, c, t)
    from_way = remote(via, result.at[c], v_send, o_sem.at[c], 6, tm)

    def send_out(g):
        far, near = outs[g]

        @pl.when(away[g])
        def _():
            far.start()

        @pl.when(jnp.logical_not(away[g]))
        def _():
            near.start()

    def first_rows(k, row, n, start):
        base = (HALO, FAR, FAR - ROWS)[k]
        return remote(relay.at[pl.ds(row, n)], ha.at[0, pl.ds(pl.multiple_of(base + start, 16), n)],
                      init_send.at[k], a_sem.at[0, k], c, ahead(k))

    first = x * QUARTER
    quarter.wait_recv()

    @pl.when(x == 0)
    def _():
        pltpu.make_async_copy(relay, ha.at[0, pl.ds(HALO, QUARTER)], a_sem.at[0, 0]).start()
        first_rows(1, 0, QUARTER, 0).start()

    @pl.when(x > 0)
    def _():
        first_rows(0, 0, QUARTER, first).start()
        first_rows(1, 0, QUARTER, first).start()

    @pl.when(x == 1)
    def _():
        first_rows(2, 16, QUARTER - 16, QUARTER + 16).start()

    @pl.when(x > 1)
    def _():
        first_rows(2, 0, QUARTER, first).start()

    def wait_start(k):
        rows = (pl.ds(HALO, ROWS), pl.ds(FAR, ROWS), pl.ds(0, FAR))[k]
        pltpu.make_async_copy(ha.at[0, rows], ha.at[0, rows], a_sem.at[0, k]).wait()

    seen1 = jnp.where(t >= 1, 1.0, 0.0).astype(jnp.float32)
    seen2 = jnp.where(t >= 2, 1.0, 0.0).astype(jnp.float32)

    def tasks(g, todo):
        for layer, first, last in todo:
            d = SPANS[layer]
            for lo, hi in pieces(first, last):
                at, n = lo + HALO, hi - lo
                if layer == 0:
                    taps = [h0f[pl.ds(at - 2, n), :].astype(jnp.bfloat16),
                            h0f[pl.ds(at - 1, n), :].astype(jnp.bfloat16),
                            ha[g, pl.ds(at, n), :]]
                    before = h0f
                else:
                    src = xb.at[layer - 1]
                    taps = [src[pl.ds(at - 2 * d, n), :], src[pl.ds(at - d, n), :], src[pl.ds(at, n), :]]
                    before = hbuf
                post = dense(taps, g, layer, hi > 0)
                h = before[pl.ds(at, n), :] + post[:, :C]
                hbuf[pl.ds(at, n), :] = h
                for begin, end, seen in ((-HALO, -ROWS, seen2), (-ROWS, 0, seen1), (0, ROWS, None)):
                    i, j = max(begin, lo), min(end, hi)
                    if i >= j:
                        continue
                    part = h[i - lo:j - lo]
                    if seen is not None:
                        part = part * seen
                    else:
                        s = post[i - lo:j - lo, C:]
                        if layer > 0 or g > 0:
                            s = s + sk[pl.ds(i, j - i), :]
                        sk[pl.ds(i, j - i), :] = s
                    if layer < 3:
                        xb[layer, pl.ds(i + HALO, j - i), :] = part.astype(jnp.bfloat16)
                    else:
                        xo[g, pl.ds(i, j - i), :] = part.astype(jnp.bfloat16)

    def last_layer(g):
        for cp in b_copies[g]:
            cp.wait_recv()

        @pl.when(t < 4)
        def _():
            xback[g, 1] = jnp.zeros((ROWS, C), jnp.bfloat16)

        @pl.when(t < 2)
        def _():
            xback[g, 0] = jnp.zeros((ROWS, C), jnp.bfloat16)

        for lo, hi in pieces(0, ROWS):
            rows = pl.ds(lo, hi - lo)
            post = dense([xback[g, 1, rows, :], xback[g, 0, rows, :], xo[g, rows, :]], g, 4, True)
            h = (hbuf[pl.ds(lo + HALO, hi - lo), :] + post[:, :C]).astype(jnp.bfloat16)
            if g == 0:
                ha[1, pl.ds(HALO + lo, hi - lo), :] = h
            else:
                hend[rows, :] = h
            skip = sk[rows, :] + post[:, C:]
            sk[rows, :] = skip
            made[g, 0, rows, :] = h
            made[g, 1, rows, :] = skip.astype(jnp.bfloat16)
        if g == 0:
            for cp in inner[1:]:
                cp.start()
        else:
            @pl.when(x < 3)
            def _():
                for cp in hand:
                    cp.start()

    def widen(g, lo, n):
        h0f[pl.ds(lo, n), :] = ha[g, pl.ds(lo, n), :].astype(jnp.float32)

    for g in range(2):
        def wait_halo(k):
            if g == 0:
                wait_start(k)
            else:
                inner[k].wait_recv()

        for layer in range(LAYERS - 1):
            wait_weights(g, layer)
        if g == 0:
            wait_start(0)
        widen(g, HALO, ROWS)
        tasks(g, OWN)

        wait_halo(1)
        wait_halo(2)
        if g == 0:
            @pl.when(x > 0)
            def _():
                pl.semaphore_signal(taken, inc=1, device_id=(section - 2, tm), device_id_type=MESH)

        @pl.when(t == 0)
        def _():
            ha[g, pl.ds(0, HALO), :] = jnp.zeros((HALO, C), jnp.bfloat16)

        @pl.when(t == 1)
        def _():
            ha[g, pl.ds(0, FAR), :] = jnp.zeros((FAR, C), jnp.bfloat16)

        widen(g, 0, HALO)
        tasks(g, AFTER)
        for cp in b_copies[g]:
            cp.start()
        wait_weights(g, 4)
        if g == 0:
            @pl.when(x > 0)
            def _():
                skip_hand.wait_recv()
                sk[...] += skin[...].astype(jnp.float32)
        last_layer(g)
        if g == 0:
            @pl.when(x == 3)
            def _():
                to_way.start()

    @pl.when(x < 3)
    def _():
        for cp in hand:
            cp.wait_send()
        skip_hand.start()
        skip_hand.wait_send()
        pl.semaphore_wait(taken, 1)
        pl.semaphore_signal(done, inc=1, device_id=(x * 2 + other, tm), device_id_type=MESH)
        pl.semaphore_wait(done, 1)
        send_out(0)

    send_out(1)
    for m in range(2):
        pltpu.make_async_copy(made.at[0], result.at[m], o_sem.at[m]).wait()

    @pl.when(x == 0)
    def _():
        to_way.wait_recv()
        from_way.start()
        from_way.wait_send()

    @pl.when(x == 3)
    def _():
        to_way.wait_send()

    quarter.wait_send()

    @pl.when(x > 0)
    def _():
        first_rows(0, 0, QUARTER, first).wait_send()

    first_rows(1, 0, QUARTER, first).wait_send()

    @pl.when(x == 1)
    def _():
        first_rows(2, 16, QUARTER - 16, QUARTER + 16).wait_send()

    @pl.when(x > 1)
    def _():
        first_rows(2, 0, QUARTER, first).wait_send()

    for g in range(2):
        @pl.when(jnp.logical_and(away[g], jnp.logical_or(x < 3, g == 1)))
        def _():
            outs[g][0].wait_send()

    for cp in w_copies:
        cp.wait_send()
    for cp in inner[1:]:
        cp.wait_send()
    for g in range(2):
        for cp in b_copies[g]:
            cp.wait_send()


def shards(signal, conv_weight, conv_bias, out_weight, out_bias):
    bf16, f32 = jnp.bfloat16, jnp.float32
    any_space = pl.BlockSpec(memory_space=pl.ANY)
    vmem = pl.BlockSpec(memory_space=pltpu.VMEM)
    dma = pltpu.SemaphoreType.DMA
    result = pl.pallas_call(
        kernel,
        out_shape=jax.ShapeDtypeStruct((2, 2, ROWS, C), bf16),
        in_specs=[any_space] * 5,
        out_specs=vmem,
        scratch_shapes=[
            pltpu.VMEM((2, LAYERS, 3 * C, 2 * C), bf16),
            pltpu.VMEM((2, LAYERS, C, 2 * C), bf16),
            pltpu.VMEM((2, LAYERS, 1, 2 * C), f32),
            pltpu.VMEM((2, LAYERS, 1, 2 * C), f32),
            pltpu.VMEM((2, SPAN, C), bf16),
            pltpu.VMEM((SPAN, C), f32),
            pltpu.VMEM((SPAN, C), f32),
            pltpu.VMEM((3, SPAN, C), bf16),
            pltpu.VMEM((2, ROWS, C), bf16),
            pltpu.VMEM((2, 2, ROWS, C), bf16),
            pltpu.VMEM((ROWS, C), bf16),
            pltpu.VMEM((ROWS, C), f32),
            pltpu.VMEM((ROWS, C), bf16),
            pltpu.VMEM((2, 2, ROWS, C), bf16),
            pltpu.VMEM((QUARTER, C), bf16),
            pltpu.VMEM((2, ROWS, C), bf16),
            dma((12,)), dma((2, 12)),
            dma((3,)), dma((2, 3)),
            dma, dma, dma((3,)),
            dma((2, 2)), dma((2, 2)),
            dma((3,)), dma, dma,
            dma((2,)), dma((2,)), dma, dma,
            pltpu.SemaphoreType.REGULAR, pltpu.SemaphoreType.REGULAR,
        ],
        compiler_params=pltpu.CompilerParams(
            collective_id=0, has_side_effects=True, vmem_limit_bytes=63 * 1024 * 1024),
        cost_estimate=pl.CostEstimate(flops=2 * 2336 * 262144, bytes_accessed=4_000_000, transcendentals=2 * 2336 * 256),
    )(signal, conv_weight, conv_bias.reshape(LAYERS, 1, 2 * C), out_weight, out_bias.reshape(LAYERS, 1, 2 * C))
    return result[None, :, 0], result[None, :, 1].astype(f32)


def solution(mesh):
    return jax.shard_map(
        shards,
        mesh=mesh,
        in_specs=(
            P(None, "tm", None),
            P("section", None, None, None),
            P("section", None, None),
            P("section", None, None, None),
            P("section", None, None),
        ),
        out_specs=(P("section", None, "tm", None), P("section", None, "tm", None)),
        check_vma=False,
    )
```

```python
import jax
import jax.numpy as jnp
from jax import lax
from jax.experimental import pallas as pl
from jax.experimental.pallas import tpu as pltpu
from jax.sharding import PartitionSpec as P

MESH = pl.DeviceIdType.MESH
C = 128
ROWS = 256
NB = 64
FAR = 176
HALO = FAR + ROWS
SPAN = HALO + ROWS
LAYERS = 5
SPANS = (1, 16, 64, 128, 512)
QUARTER = 64
CHUNK = 256
OWN = ((0, 16, ROWS), (1, 48, ROWS), (2, 176, ROWS))
AFTER = ((0, -416, 16), (1, -384, 48), (2, -256, 176), (3, 0, ROWS))


def pieces(lo, hi):
    count = -(-(hi - lo) // CHUNK)
    size = -(-(hi - lo) // (16 * count)) * 16
    return [(at, min(at + size, hi)) for at in range(lo, hi, size)]


def kernel(signal, conv_w, conv_b, out_w, out_b, result,
           wc, wo, bc, bo, ha, h0f, hbuf, xb, xo, xback, hend, sk, skin, made, relay,
           wsend, wsem, a_send, a_sem, r_send, r_sem, init_send, b_send, b_sem, h_send, s_send, s_sem,
           o_send, o_sem, done, taken, turn):
    section = lax.axis_index("section")
    tm = lax.axis_index("tm")
    x, c = section // 2, section % 2
    y, z = tm // 16, tm % 16
    turned = (y + 3 + c) % 4
    pos = z * 4 + (turned ^ (turned >> 1))
    t = jnp.where(c == 1, pos, NB - 1 - pos)
    step = 2 * c - 1

    def tm_of(p, rec):
        n = p % 4
        return (((n ^ (n >> 1)) + 1 - rec) % 4) * 16 + p // 4

    def ahead(k):
        return tm_of((pos + step * k + NB) % NB, c)

    def worker(block, rec):
        return tm_of(jnp.where(rec == 1, block, NB - 1 - block), rec)

    other = 1 - c
    mine = jnp.where(tm == t, 1, 0)

    barrier = pltpu.get_barrier_semaphore()

    def greet(sec, where):
        pl.semaphore_signal(barrier, inc=1, device_id=(sec, where), device_id_type=MESH)

    greet(x * 2 + other, tm)
    for k in (1, 2, 4):
        greet(section, ahead(-k))

    @pl.when(x > 0)
    def _():
        for k in range(3):
            greet(section - 2, ahead(-k))

    greet(x * 2 + other, t)

    @pl.when(x == 0)
    def _():
        for plane in range(4):
            for k in range(3):
                if plane > 0 or k == 1:
                    greet(plane * 2 + c, ahead(-k))

    for m in range(2):
        @pl.when(jnp.logical_or(c != m, tm != worker(tm, m)))
        def _():
            greet(x * 2 + m, worker(tm, m))

    pl.semaphore_wait(barrier, 7 - mine + jnp.where(x < 3, 3, 0) + jnp.where(x == 0, 1, 3))

    def remote(src, dst, send, recv, sec, where):
        return pltpu.make_async_remote_copy(
            src_ref=src, dst_ref=dst, send_sem=send, recv_sem=recv,
            device_id=(sec, where), device_id_type=MESH)

    quarter = remote(signal.at[other, pl.ds(pl.multiple_of(x * QUARTER, QUARTER), QUARTER)], relay, r_send, r_sem,
                     x * 2 + other, worker(tm, other))
    quarter.start()

    parts = ((0, ROWS, HALO), (0, ROWS, FAR), (ROWS - FAR, FAR, 0))

    def start_copies(g, src, sends, sec):
        return [remote(src.at[pl.ds(lo, n)], ha.at[g, pl.ds(at, n)], sends.at[k], a_sem.at[g, k], sec, ahead(k))
                for k, (lo, n, at) in enumerate(parts)]

    jobs = []
    for layer in range(LAYERS):
        jobs.append((conv_w.at[0, layer], lambda g, l=layer: wc.at[g, l]))
        jobs.append((out_w.at[0, layer], lambda g, l=layer: wo.at[g, l]))
        if layer == 0:
            jobs.append((conv_b, lambda g: bc.at[g]))
            jobs.append((out_b, lambda g: bo.at[g]))
    w_copies = []
    for i, (src, dst) in enumerate(jobs):
        cp = remote(src, dst(c), wsend.at[i], wsem.at[c, i], x * 2 + other, tm)
        cp.start()
        w_copies.append(cp)
        pltpu.make_async_copy(src, dst(c), wsem.at[c, i]).start()
    need = {0: (0, 1, 2, 3), 1: (4, 5), 2: (6, 7), 3: (8, 9), 4: (10, 11)}

    def wait_weights(g, layer):
        for i in need[layer]:
            src, dst = jobs[i]
            pltpu.make_async_copy(src, dst(g), wsem.at[g, i]).wait()

    def dense(taps, g, layer, own):
        pre = jnp.dot(jnp.concatenate(taps, axis=1), wc[g, layer],
                      preferred_element_type=jnp.float32) + bc[g, layer]
        pre = pre.astype(jnp.bfloat16)
        half = jnp.bfloat16(0.5)
        gated = jnp.tanh(pre[:, :C]) * (half * jnp.tanh(half * pre[:, C:]) + half)
        if own:
            return jnp.dot(gated, wo[g, layer], preferred_element_type=jnp.float32) + bo[g, layer]
        return (jnp.dot(gated, wo[g, layer, :, pl.ds(0, C)], preferred_element_type=jnp.float32)
                + bo[g, layer, :, pl.ds(0, C)])

    next_section = jnp.where(x < 3, section + 2, section - 6)
    hand = start_copies(0, hend, h_send, next_section)
    skip_hand = remote(made.at[1, 1], skin, s_send, s_sem, next_section, ahead(0))
    inner = start_copies(1, ha.at[1, pl.ds(HALO, ROWS)], a_send, section)
    b_copies = [[remote(xo.at[g], xback.at[g, i], b_send.at[g, i], b_sem.at[g, i], section, ahead(k))
                 for i, k in enumerate((2, 4))] for g in range(2)]
    away = [jnp.logical_or(c != g, mine == 0) for g in range(2)]
    outs = [(remote(made.at[g], result.at[c], o_send.at[g], o_sem.at[c], x * 2 + g, t),
             pltpu.make_async_copy(made.at[g], result.at[c], o_sem.at[c])) for g in range(2)]

    def send_out(g):
        far, near = outs[g]

        @pl.when(away[g])
        def _():
            far.start()

        @pl.when(jnp.logical_not(away[g]))
        def _():
            near.start()

    def first_rows(k, row, n, start):
        base = (HALO, FAR, FAR - ROWS)[k]
        return remote(relay.at[pl.ds(row, n)], ha.at[0, pl.ds(pl.multiple_of(base + start, 16), n)],
                      init_send.at[k], a_sem.at[0, k], c, ahead(k))

    first = x * QUARTER
    quarter.wait_recv()

    @pl.when(c == 1)
    def _():
        pl.semaphore_wait(turn, 1)

    @pl.when(x == 0)
    def _():
        pltpu.make_async_copy(relay, ha.at[0, pl.ds(HALO, QUARTER)], a_sem.at[0, 0]).start()
        first_rows(1, 0, QUARTER, 0).start()

    @pl.when(x > 0)
    def _():
        first_rows(0, 0, QUARTER, first).start()
        first_rows(1, 0, QUARTER, first).start()

    @pl.when(x == 1)
    def _():
        first_rows(2, 16, QUARTER - 16, QUARTER + 16).start()
        first_rows(2, 16, QUARTER - 16, QUARTER + 16).wait_send()

    @pl.when(x > 1)
    def _():
        first_rows(2, 0, QUARTER, first).start()
        first_rows(2, 0, QUARTER, first).wait_send()

    @pl.when(x > 0)
    def _():
        first_rows(0, 0, QUARTER, first).wait_send()

    first_rows(1, 0, QUARTER, first).wait_send()

    @pl.when(c == 0)
    def _():
        pl.semaphore_signal(turn, inc=1, device_id=(x * 2 + other, tm), device_id_type=MESH)

    def wait_start(k):
        rows = (pl.ds(HALO, ROWS), pl.ds(FAR, ROWS), pl.ds(0, FAR))[k]
        pltpu.make_async_copy(ha.at[0, rows], ha.at[0, rows], a_sem.at[0, k]).wait()

    seen1 = jnp.where(t >= 1, 1.0, 0.0).astype(jnp.float32)
    seen2 = jnp.where(t >= 2, 1.0, 0.0).astype(jnp.float32)

    def tasks(g, todo):
        for layer, first, last in todo:
            d = SPANS[layer]
            for lo, hi in pieces(first, last):
                at, n = lo + HALO, hi - lo
                if layer == 0:
                    taps = [h0f[pl.ds(at - 2, n), :].astype(jnp.bfloat16),
                            h0f[pl.ds(at - 1, n), :].astype(jnp.bfloat16),
                            ha[g, pl.ds(at, n), :]]
                    before = h0f
                else:
                    src = xb.at[layer - 1]
                    taps = [src[pl.ds(at - 2 * d, n), :], src[pl.ds(at - d, n), :], src[pl.ds(at, n), :]]
                    before = hbuf
                post = dense(taps, g, layer, hi > 0)
                h = before[pl.ds(at, n), :] + post[:, :C]
                hbuf[pl.ds(at, n), :] = h
                for begin, end, seen in ((-HALO, -ROWS, seen2), (-ROWS, 0, seen1), (0, ROWS, None)):
                    i, j = max(begin, lo), min(end, hi)
                    if i >= j:
                        continue
                    part = h[i - lo:j - lo]
                    if seen is not None:
                        part = part * seen
                    else:
                        s = post[i - lo:j - lo, C:]
                        if layer > 0 or g > 0:
                            s = s + sk[pl.ds(i, j - i), :]
                        sk[pl.ds(i, j - i), :] = s
                    if layer < 3:
                        xb[layer, pl.ds(i + HALO, j - i), :] = part.astype(jnp.bfloat16)
                    else:
                        xo[g, pl.ds(i, j - i), :] = part.astype(jnp.bfloat16)

    def last_layer(g):
        for cp in b_copies[g]:
            cp.wait_recv()

        @pl.when(t < 4)
        def _():
            xback[g, 1] = jnp.zeros((ROWS, C), jnp.bfloat16)

        @pl.when(t < 2)
        def _():
            xback[g, 0] = jnp.zeros((ROWS, C), jnp.bfloat16)

        for lo, hi in pieces(0, ROWS):
            rows = pl.ds(lo, hi - lo)
            post = dense([xback[g, 1, rows, :], xback[g, 0, rows, :], xo[g, rows, :]], g, 4, True)
            h = (hbuf[pl.ds(lo + HALO, hi - lo), :] + post[:, :C]).astype(jnp.bfloat16)
            if g == 0:
                ha[1, pl.ds(HALO + lo, hi - lo), :] = h
            else:
                hend[rows, :] = h
            skip = sk[rows, :] + post[:, C:]
            sk[rows, :] = skip
            made[g, 0, rows, :] = h
            made[g, 1, rows, :] = skip.astype(jnp.bfloat16)
        if g == 0:
            for cp in inner[1:]:
                cp.start()
        else:
            @pl.when(x < 3)
            def _():
                for cp in hand:
                    cp.start()

    def widen(g, lo, n):
        h0f[pl.ds(lo, n), :] = ha[g, pl.ds(lo, n), :].astype(jnp.float32)

    for g in range(2):
        def wait_halo(k):
            if g == 0:
                wait_start(k)
            else:
                inner[k].wait_recv()

        for layer in range(LAYERS - 1):
            wait_weights(g, layer)
        if g == 0:
            wait_start(0)
        widen(g, HALO, ROWS)
        tasks(g, OWN)

        wait_halo(1)
        wait_halo(2)
        if g == 0:
            @pl.when(x > 0)
            def _():
                pl.semaphore_signal(taken, inc=1, device_id=(section - 2, tm), device_id_type=MESH)

        @pl.when(t == 0)
        def _():
            ha[g, pl.ds(0, HALO), :] = jnp.zeros((HALO, C), jnp.bfloat16)

        @pl.when(t == 1)
        def _():
            ha[g, pl.ds(0, FAR), :] = jnp.zeros((FAR, C), jnp.bfloat16)

        widen(g, 0, HALO)
        tasks(g, AFTER)
        for cp in b_copies[g]:
            cp.start()
        wait_weights(g, 4)
        if g == 0:
            @pl.when(x > 0)
            def _():
                skip_hand.wait_recv()
                sk[...] += skin[...].astype(jnp.float32)
        last_layer(g)
        if g == 0:
            @pl.when(x == 3)
            def _():
                send_out(0)

    @pl.when(x < 3)
    def _():
        for cp in hand:
            cp.wait_send()
        skip_hand.start()
        skip_hand.wait_send()
        pl.semaphore_wait(taken, 1)
        pl.semaphore_signal(done, inc=1, device_id=(x * 2 + other, tm), device_id_type=MESH)
        pl.semaphore_wait(done, 1)
        send_out(0)

    send_out(1)
    for m in range(2):
        pltpu.make_async_copy(made.at[0], result.at[m], o_sem.at[m]).wait()

    quarter.wait_send()

    for g in range(2):
        @pl.when(away[g])
        def _():
            outs[g][0].wait_send()

    for cp in w_copies:
        cp.wait_send()
    for cp in inner[1:]:
        cp.wait_send()
    for g in range(2):
        for cp in b_copies[g]:
            cp.wait_send()


def shards(signal, conv_weight, conv_bias, out_weight, out_bias):
    bf16, f32 = jnp.bfloat16, jnp.float32
    any_space = pl.BlockSpec(memory_space=pl.ANY)
    vmem = pl.BlockSpec(memory_space=pltpu.VMEM)
    dma = pltpu.SemaphoreType.DMA
    result = pl.pallas_call(
        kernel,
        out_shape=jax.ShapeDtypeStruct((2, 2, ROWS, C), bf16),
        in_specs=[any_space] * 5,
        out_specs=vmem,
        scratch_shapes=[
            pltpu.VMEM((2, LAYERS, 3 * C, 2 * C), bf16),
            pltpu.VMEM((2, LAYERS, C, 2 * C), bf16),
            pltpu.VMEM((2, LAYERS, 1, 2 * C), f32),
            pltpu.VMEM((2, LAYERS, 1, 2 * C), f32),
            pltpu.VMEM((2, SPAN, C), bf16),
            pltpu.VMEM((SPAN, C), f32),
            pltpu.VMEM((SPAN, C), f32),
            pltpu.VMEM((3, SPAN, C), bf16),
            pltpu.VMEM((2, ROWS, C), bf16),
            pltpu.VMEM((2, 2, ROWS, C), bf16),
            pltpu.VMEM((ROWS, C), bf16),
            pltpu.VMEM((ROWS, C), f32),
            pltpu.VMEM((ROWS, C), bf16),
            pltpu.VMEM((2, 2, ROWS, C), bf16),
            pltpu.VMEM((QUARTER, C), bf16),
            dma((12,)), dma((2, 12)),
            dma((3,)), dma((2, 3)),
            dma, dma, dma((3,)),
            dma((2, 2)), dma((2, 2)),
            dma((3,)), dma, dma,
            dma((2,)), dma((2,)),
            pltpu.SemaphoreType.REGULAR, pltpu.SemaphoreType.REGULAR, pltpu.SemaphoreType.REGULAR,
        ],
        compiler_params=pltpu.CompilerParams(
            collective_id=0, has_side_effects=True, vmem_limit_bytes=63 * 1024 * 1024),
        cost_estimate=pl.CostEstimate(flops=2 * 2336 * 262144, bytes_accessed=4_000_000, transcendentals=2 * 2336 * 256),
    )(signal, conv_weight, conv_bias.reshape(LAYERS, 1, 2 * C), out_weight, out_bias.reshape(LAYERS, 1, 2 * C))
    return result[None, :, 0], result[None, :, 1].astype(f32)


def solution(mesh):
    return jax.shard_map(
        shards,
        mesh=mesh,
        in_specs=(
            P(None, "tm", None),
            P("section", None, None, None),
            P("section", None, None),
            P("section", None, None, None),
            P("section", None, None),
        ),
        out_specs=(P("section", None, "tm", None), P("section", None, "tm", None)),
        check_vma=False,
    )
```

```python
import jax
import jax.numpy as jnp
from jax import lax
from jax.experimental import pallas as pl
from jax.experimental.pallas import tpu as pltpu
from jax.sharding import PartitionSpec as P

MESH = pl.DeviceIdType.MESH
C = 128
ROWS = 256
NB = 64
FAR = 176
HALO = FAR + ROWS
SPAN = HALO + ROWS
LAYERS = 5
SPANS = (1, 16, 64, 128, 512)
QUARTER = 64
CHUNK = 256
OWN = ((0, 16, ROWS), (1, 48, ROWS), (2, 176, ROWS))
AFTER = ((0, -416, 16), (1, -384, 48), (2, -256, 176), (3, 0, ROWS))


def pieces(lo, hi):
    count = -(-(hi - lo) // CHUNK)
    size = -(-(hi - lo) // (16 * count)) * 16
    return [(at, min(at + size, hi)) for at in range(lo, hi, size)]


def kernel(signal, conv_w, conv_b, out_w, out_b, result,
           wc, wo, bc, bo, ha, h0f, hbuf, xb, xo, xback, hend, sk, gs, skin, made, relay,
           wsend, wsem, a_send, a_sem, r_send, r_sem, init_send, b_send, b_sem, h_send, s_send, s_sem,
           o_send, o_sem, done, taken):
    section = lax.axis_index("section")
    tm = lax.axis_index("tm")
    x, c = section // 2, section % 2
    y, z = tm // 16, tm % 16
    turned = (y + 3 + c) % 4
    pos = z * 4 + (turned ^ (turned >> 1))
    t = jnp.where(c == 1, pos, NB - 1 - pos)
    step = 2 * c - 1

    def tm_of(p, rec):
        n = p % 4
        return (((n ^ (n >> 1)) + 1 - rec) % 4) * 16 + p // 4

    def ahead(k):
        return tm_of((pos + step * k + NB) % NB, c)

    def worker(block, rec):
        return tm_of(jnp.where(rec == 1, block, NB - 1 - block), rec)

    other = 1 - c
    mine = jnp.where(tm == t, 1, 0)

    barrier = pltpu.get_barrier_semaphore()

    def greet(sec, where):
        pl.semaphore_signal(barrier, inc=1, device_id=(sec, where), device_id_type=MESH)

    greet(x * 2 + other, tm)
    for k in (1, 2, 4):
        greet(section, ahead(-k))

    @pl.when(x > 0)
    def _():
        for k in range(3):
            greet(section - 2, ahead(-k))

    greet(x * 2 + other, t)

    @pl.when(x == 0)
    def _():
        for plane in range(4):
            for k in range(3):
                if plane > 0 or k == 1:
                    greet(plane * 2 + c, ahead(-k))

    for m in range(2):
        @pl.when(jnp.logical_or(c != m, tm != worker(tm, m)))
        def _():
            greet(x * 2 + m, worker(tm, m))

    pl.semaphore_wait(barrier, 7 - mine + jnp.where(x < 3, 3, 0) + jnp.where(x == 0, 1, 3))

    def remote(src, dst, send, recv, sec, where):
        return pltpu.make_async_remote_copy(
            src_ref=src, dst_ref=dst, send_sem=send, recv_sem=recv,
            device_id=(sec, where), device_id_type=MESH)

    quarter = remote(signal.at[other, pl.ds(pl.multiple_of(x * QUARTER, QUARTER), QUARTER)], relay, r_send, r_sem,
                     x * 2 + other, worker(tm, other))
    quarter.start()

    parts = ((0, ROWS, HALO), (0, ROWS, FAR), (ROWS - FAR, FAR, 0))

    def start_copies(g, src, sends, sec):
        return [remote(src.at[pl.ds(lo, n)], ha.at[g, pl.ds(at, n)], sends.at[k], a_sem.at[g, k], sec, ahead(k))
                for k, (lo, n, at) in enumerate(parts)]

    jobs = []
    for layer in range(LAYERS):
        jobs.append((conv_w.at[0, layer], lambda g, l=layer: wc.at[g, l]))
        jobs.append((out_w.at[0, layer], lambda g, l=layer: wo.at[g, l]))
        if layer == 0:
            jobs.append((conv_b, lambda g: bc.at[g]))
            jobs.append((out_b, lambda g: bo.at[g]))
    w_copies = []
    for i, (src, dst) in enumerate(jobs):
        cp = remote(src, dst(c), wsend.at[i], wsem.at[c, i], x * 2 + other, tm)
        cp.start()
        w_copies.append(cp)
        pltpu.make_async_copy(src, dst(c), wsem.at[c, i]).start()
    need = {0: (0, 1, 2, 3), 1: (4, 5), 2: (6, 7), 3: (8, 9), 4: (10, 11)}

    def wait_weights(g, layer):
        for i in need[layer]:
            src, dst = jobs[i]
            pltpu.make_async_copy(src, dst(g), wsem.at[g, i]).wait()

    def dense(taps, g, layer):
        pre = jnp.dot(jnp.concatenate(taps, axis=1), wc[g, layer],
                      preferred_element_type=jnp.float32) + bc[g, layer]
        pre = pre.astype(jnp.bfloat16)
        half = jnp.bfloat16(0.5)
        gated = jnp.tanh(pre[:, :C]) * (half * jnp.tanh(half * pre[:, C:]) + half)
        res = (jnp.dot(gated, wo[g, layer, :, pl.ds(0, C)], preferred_element_type=jnp.float32)
               + bo[g, layer, :, pl.ds(0, C)])
        return gated, res

    def skip_part(g, layers):
        weights = [wo[g, layer, :, pl.ds(C, C)] for layer in layers]
        out = jnp.dot(jnp.concatenate([gs[layer] for layer in layers], axis=1), jnp.concatenate(weights, axis=0),
                      preferred_element_type=jnp.float32)
        for layer in layers:
            out = out + bo[g, layer, :, pl.ds(C, C)]
        return out

    next_section = jnp.where(x < 3, section + 2, section - 6)
    hand = start_copies(0, hend, h_send, next_section)
    skip_hand = remote(made.at[1, 1], skin, s_send, s_sem, next_section, ahead(0))
    inner = start_copies(1, ha.at[1, pl.ds(HALO, ROWS)], a_send, section)
    b_copies = [[remote(xo.at[g], xback.at[g, i], b_send.at[g, i], b_sem.at[g, i], section, ahead(k))
                 for i, k in enumerate((2, 4))] for g in range(2)]
    away = [jnp.logical_or(c != g, mine == 0) for g in range(2)]
    outs = [(remote(made.at[g], result.at[c], o_send.at[g], o_sem.at[c], x * 2 + g, t),
             pltpu.make_async_copy(made.at[g], result.at[c], o_sem.at[c])) for g in range(2)]

    def send_out(g):
        far, near = outs[g]

        @pl.when(away[g])
        def _():
            far.start()

        @pl.when(jnp.logical_not(away[g]))
        def _():
            near.start()

    def first_rows(k, row, n, start):
        base = (HALO, FAR, FAR - ROWS)[k]
        return remote(relay.at[pl.ds(row, n)], ha.at[0, pl.ds(pl.multiple_of(base + start, 16), n)],
                      init_send.at[k], a_sem.at[0, k], c, ahead(k))

    first = x * QUARTER
    quarter.wait_recv()

    @pl.when(x == 0)
    def _():
        pltpu.make_async_copy(relay, ha.at[0, pl.ds(HALO, QUARTER)], a_sem.at[0, 0]).start()
        first_rows(1, 0, QUARTER, 0).start()

    @pl.when(x > 0)
    def _():
        first_rows(0, 0, QUARTER, first).start()
        first_rows(1, 0, QUARTER, first).start()

    @pl.when(x == 1)
    def _():
        first_rows(2, 16, QUARTER - 16, QUARTER + 16).start()

    @pl.when(x > 1)
    def _():
        first_rows(2, 0, QUARTER, first).start()

    def wait_start(k):
        rows = (pl.ds(HALO, ROWS), pl.ds(FAR, ROWS), pl.ds(0, FAR))[k]
        pltpu.make_async_copy(ha.at[0, rows], ha.at[0, rows], a_sem.at[0, k]).wait()

    seen1 = jnp.where(t >= 1, 1.0, 0.0).astype(jnp.float32)
    seen2 = jnp.where(t >= 2, 1.0, 0.0).astype(jnp.float32)

    def tasks(g, todo):
        for layer, first, last in todo:
            d = SPANS[layer]
            for lo, hi in pieces(first, last):
                at, n = lo + HALO, hi - lo
                if layer == 0:
                    taps = [h0f[pl.ds(at - 2, n), :].astype(jnp.bfloat16),
                            h0f[pl.ds(at - 1, n), :].astype(jnp.bfloat16),
                            ha[g, pl.ds(at, n), :]]
                    before = h0f
                else:
                    src = xb.at[layer - 1]
                    taps = [src[pl.ds(at - 2 * d, n), :], src[pl.ds(at - d, n), :], src[pl.ds(at, n), :]]
                    before = hbuf
                gated, res = dense(taps, g, layer)
                h = before[pl.ds(at, n), :] + res
                hbuf[pl.ds(at, n), :] = h
                for begin, end, seen in ((-HALO, -ROWS, seen2), (-ROWS, 0, seen1), (0, ROWS, None)):
                    i, j = max(begin, lo), min(end, hi)
                    if i >= j:
                        continue
                    part = h[i - lo:j - lo]
                    if seen is not None:
                        part = part * seen
                    else:
                        gs[layer, pl.ds(i, j - i), :] = gated[i - lo:j - lo]
                    if layer < 3:
                        xb[layer, pl.ds(i + HALO, j - i), :] = part.astype(jnp.bfloat16)
                    else:
                        xo[g, pl.ds(i, j - i), :] = part.astype(jnp.bfloat16)

    def last_layer(g):
        for cp in b_copies[g]:
            cp.wait_recv()

        @pl.when(t < 4)
        def _():
            xback[g, 1] = jnp.zeros((ROWS, C), jnp.bfloat16)

        @pl.when(t < 2)
        def _():
            xback[g, 0] = jnp.zeros((ROWS, C), jnp.bfloat16)

        for lo, hi in pieces(0, ROWS):
            rows = pl.ds(lo, hi - lo)
            gated, res = dense([xback[g, 1, rows, :], xback[g, 0, rows, :], xo[g, rows, :]], g, 4)
            h = (hbuf[pl.ds(lo + HALO, hi - lo), :] + res).astype(jnp.bfloat16)
            gs[4, rows, :] = gated
            if g == 0:
                ha[1, pl.ds(HALO + lo, hi - lo), :] = h
            else:
                hend[rows, :] = h
        if g == 0:
            for cp in inner[1:]:
                cp.start()
        else:
            @pl.when(x < 3)
            def _():
                for cp in hand:
                    cp.start()

        skip = sk[...] + skip_part(g, (4,))
        sk[...] = skip
        made[g, 0] = ha[1, pl.ds(HALO, ROWS), :] if g == 0 else hend[...]
        made[g, 1] = skip.astype(jnp.bfloat16)

    def widen(g, lo, n):
        h0f[pl.ds(lo, n), :] = ha[g, pl.ds(lo, n), :].astype(jnp.float32)

    for g in range(2):
        def wait_halo(k):
            if g == 0:
                wait_start(k)
            else:
                inner[k].wait_recv()

        for layer in range(LAYERS - 1):
            wait_weights(g, layer)
        if g == 0:
            wait_start(0)
        widen(g, HALO, ROWS)
        tasks(g, OWN)

        wait_halo(1)
        wait_halo(2)
        if g == 0:
            @pl.when(x > 0)
            def _():
                pl.semaphore_signal(taken, inc=1, device_id=(section - 2, tm), device_id_type=MESH)

        @pl.when(t == 0)
        def _():
            ha[g, pl.ds(0, HALO), :] = jnp.zeros((HALO, C), jnp.bfloat16)

        @pl.when(t == 1)
        def _():
            ha[g, pl.ds(0, FAR), :] = jnp.zeros((FAR, C), jnp.bfloat16)

        widen(g, 0, HALO)
        tasks(g, AFTER)
        for cp in b_copies[g]:
            cp.start()
        wait_weights(g, 4)
        if g == 0:
            sk[...] = skip_part(g, range(4))
        else:
            sk[...] += skip_part(g, range(4))
        if g == 0:
            @pl.when(x > 0)
            def _():
                skip_hand.wait_recv()
                sk[...] += skin[...].astype(jnp.float32)
        last_layer(g)
        if g == 0:
            @pl.when(x == 3)
            def _():
                send_out(0)

    @pl.when(x < 3)
    def _():
        for cp in hand:
            cp.wait_send()
        skip_hand.start()
        skip_hand.wait_send()
        pl.semaphore_wait(taken, 1)
        pl.semaphore_signal(done, inc=1, device_id=(x * 2 + other, tm), device_id_type=MESH)
        pl.semaphore_wait(done, 1)
        send_out(0)

    send_out(1)
    for m in range(2):
        pltpu.make_async_copy(made.at[0], result.at[m], o_sem.at[m]).wait()

    quarter.wait_send()

    @pl.when(x > 0)
    def _():
        first_rows(0, 0, QUARTER, first).wait_send()

    first_rows(1, 0, QUARTER, first).wait_send()

    @pl.when(x == 1)
    def _():
        first_rows(2, 16, QUARTER - 16, QUARTER + 16).wait_send()

    @pl.when(x > 1)
    def _():
        first_rows(2, 0, QUARTER, first).wait_send()

    for g in range(2):
        @pl.when(away[g])
        def _():
            outs[g][0].wait_send()

    for cp in w_copies:
        cp.wait_send()
    for cp in inner[1:]:
        cp.wait_send()
    for g in range(2):
        for cp in b_copies[g]:
            cp.wait_send()


def shards(signal, conv_weight, conv_bias, out_weight, out_bias):
    bf16, f32 = jnp.bfloat16, jnp.float32
    any_space = pl.BlockSpec(memory_space=pl.ANY)
    vmem = pl.BlockSpec(memory_space=pltpu.VMEM)
    dma = pltpu.SemaphoreType.DMA
    result = pl.pallas_call(
        kernel,
        out_shape=jax.ShapeDtypeStruct((2, 2, ROWS, C), bf16),
        in_specs=[any_space] * 5,
        out_specs=vmem,
        scratch_shapes=[
            pltpu.VMEM((2, LAYERS, 3 * C, 2 * C), bf16),
            pltpu.VMEM((2, LAYERS, C, 2 * C), bf16),
            pltpu.VMEM((2, LAYERS, 1, 2 * C), f32),
            pltpu.VMEM((2, LAYERS, 1, 2 * C), f32),
            pltpu.VMEM((2, SPAN, C), bf16),
            pltpu.VMEM((SPAN, C), f32),
            pltpu.VMEM((SPAN, C), f32),
            pltpu.VMEM((3, SPAN, C), bf16),
            pltpu.VMEM((2, ROWS, C), bf16),
            pltpu.VMEM((2, 2, ROWS, C), bf16),
            pltpu.VMEM((ROWS, C), bf16),
            pltpu.VMEM((ROWS, C), f32),
            pltpu.VMEM((LAYERS, ROWS, C), bf16),
            pltpu.VMEM((ROWS, C), bf16),
            pltpu.VMEM((2, 2, ROWS, C), bf16),
            pltpu.VMEM((QUARTER, C), bf16),
            dma((12,)), dma((2, 12)),
            dma((3,)), dma((2, 3)),
            dma, dma, dma((3,)),
            dma((2, 2)), dma((2, 2)),
            dma((3,)), dma, dma,
            dma((2,)), dma((2,)),
            pltpu.SemaphoreType.REGULAR, pltpu.SemaphoreType.REGULAR,
        ],
        compiler_params=pltpu.CompilerParams(
            collective_id=0, has_side_effects=True, vmem_limit_bytes=63 * 1024 * 1024),
        cost_estimate=pl.CostEstimate(flops=2 * 2336 * 262144, bytes_accessed=4_000_000, transcendentals=2 * 2336 * 256),
    )(signal, conv_weight, conv_bias.reshape(LAYERS, 1, 2 * C), out_weight, out_bias.reshape(LAYERS, 1, 2 * C))
    return result[None, :, 0], result[None, :, 1].astype(f32)


def solution(mesh):
    return jax.shard_map(
        shards,
        mesh=mesh,
        in_specs=(
            P(None, "tm", None),
            P("section", None, None, None),
            P("section", None, None),
            P("section", None, None, None),
            P("section", None, None),
        ),
        out_specs=(P("section", None, "tm", None), P("section", None, "tm", None)),
        check_vma=False,
    )
```

```python
import jax
import jax.numpy as jnp
from jax import lax
from jax.experimental import pallas as pl
from jax.experimental.pallas import tpu as pltpu
from jax.sharding import PartitionSpec as P

MESH = pl.DeviceIdType.MESH
C = 128
ROWS = 256
NB = 64
FAR = 176
HALO = FAR + ROWS
SPAN = HALO + ROWS
LAYERS = 5
SPANS = (1, 16, 64, 128, 512)
CHUNK = 256
OWN = ((0, 16, ROWS), (1, 48, ROWS), (2, 176, ROWS))
AFTER = ((0, -416, 16), (1, -384, 48), (2, -256, 176), (3, 0, ROWS))


def pieces(lo, hi):
    count = -(-(hi - lo) // CHUNK)
    size = -(-(hi - lo) // (16 * count)) * 16
    return [(at, min(at + size, hi)) for at in range(lo, hi, size)]


def kernel(signal, conv_w, conv_b, out_w, out_b, result,
           wc, wo, bc, bo, ha, h0f, hbuf, xb, xo, xback, hend, sk, skin, made, relay,
           wsend, wsem, a_send, a_sem, r_send, r_sem, init_send, b_send, b_sem, h_send, s_send, s_sem,
           o_send, o_sem, done, taken):
    section = lax.axis_index("section")
    tm = lax.axis_index("tm")
    x, c = section // 2, section % 2
    y, z = tm // 16, tm % 16
    turned = (y + 3 + c) % 4
    pos = z * 4 + (turned ^ (turned >> 1))
    t = jnp.where(c == 1, pos, NB - 1 - pos)
    step = 2 * c - 1

    def tm_of(p, rec):
        n = p % 4
        return (((n ^ (n >> 1)) + 1 - rec) % 4) * 16 + p // 4

    def ahead(k):
        return tm_of((pos + step * k + NB) % NB, c)

    def worker(block, rec):
        return tm_of(jnp.where(rec == 1, block, NB - 1 - block), rec)

    other = 1 - c
    mine = jnp.where(tm == t, 1, 0)

    barrier = pltpu.get_barrier_semaphore()

    def greet(sec, where):
        pl.semaphore_signal(barrier, inc=1, device_id=(sec, where), device_id_type=MESH)

    greet(x * 2 + other, tm)
    for k in (1, 2, 4):
        greet(section, ahead(-k))

    @pl.when(x > 0)
    def _():
        for k in range(3):
            greet(section - 2, ahead(-k))

    @pl.when(x != 2)
    def _():
        greet(x * 2 + other, t)

    @pl.when(x == 0)
    def _():
        for plane in (0, 1, 3):
            for k in range(3):
                if plane > 0 or k > 0:
                    greet(plane * 2 + c, ahead(-k))

    for m in range(2):
        @pl.when(jnp.logical_or(c != m, tm != worker(tm, m)))
        def _():
            greet(x * 2 + m, worker(tm, m))

    pl.semaphore_wait(barrier, 6 - mine + jnp.where(x < 3, 3, 0) + jnp.where(x == 2, 0, jnp.where(x == 0, 3, 4)))

    def remote(src, dst, send, recv, sec, where):
        return pltpu.make_async_remote_copy(
            src_ref=src, dst_ref=dst, send_sem=send, recv_sem=recv,
            device_id=(sec, where), device_id_type=MESH)

    def moved(start, n):
        return remote(signal.at[other, pl.ds(start, n)], relay.at[pl.ds(0, n)], r_send, r_sem,
                      x * 2 + other, worker(tm, other))

    shares = ((0, 0, 128), (1, 128, 64), (3, 192, 64))
    for plane, start, n in shares:
        @pl.when(x == plane)
        def _():
            moved(start, n).start()

    parts = ((0, ROWS, HALO), (0, ROWS, FAR), (ROWS - FAR, FAR, 0))

    def start_copies(g, src, sends, sec):
        return [remote(src.at[pl.ds(lo, n)], ha.at[g, pl.ds(at, n)], sends.at[k], a_sem.at[g, k], sec, ahead(k))
                for k, (lo, n, at) in enumerate(parts)]

    jobs = []
    for layer in range(LAYERS):
        jobs.append((conv_w.at[0, layer], lambda g, l=layer: wc.at[g, l]))
        jobs.append((out_w.at[0, layer], lambda g, l=layer: wo.at[g, l]))
        if layer == 0:
            jobs.append((conv_b, lambda g: bc.at[g]))
            jobs.append((out_b, lambda g: bo.at[g]))
    w_copies = []
    for i, (src, dst) in enumerate(jobs):
        cp = remote(src, dst(c), wsend.at[i], wsem.at[c, i], x * 2 + other, tm)
        cp.start()
        w_copies.append(cp)
        pltpu.make_async_copy(src, dst(c), wsem.at[c, i]).start()
    need = {0: (0, 1, 2, 3), 1: (4, 5), 2: (6, 7), 3: (8, 9), 4: (10, 11)}

    def wait_weights(g, layer):
        for i in need[layer]:
            src, dst = jobs[i]
            pltpu.make_async_copy(src, dst(g), wsem.at[g, i]).wait()

    def dense(taps, g, layer, own):
        pre = jnp.dot(jnp.concatenate(taps, axis=1), wc[g, layer],
                      preferred_element_type=jnp.float32) + bc[g, layer]
        pre = pre.astype(jnp.bfloat16)
        half = jnp.bfloat16(0.5)
        gated = jnp.tanh(pre[:, :C]) * (half * jnp.tanh(half * pre[:, C:]) + half)
        if own:
            return jnp.dot(gated, wo[g, layer], preferred_element_type=jnp.float32) + bo[g, layer]
        return (jnp.dot(gated, wo[g, layer, :, pl.ds(0, C)], preferred_element_type=jnp.float32)
                + bo[g, layer, :, pl.ds(0, C)])

    next_section = jnp.where(x < 3, section + 2, section - 6)
    hand = start_copies(0, hend, h_send, next_section)
    skip_hand = remote(made.at[1, 1], skin, s_send, s_sem, next_section, ahead(0))
    inner = start_copies(1, ha.at[1, pl.ds(HALO, ROWS)], a_send, section)
    b_copies = [[remote(xo.at[g], xback.at[g, i], b_send.at[g, i], b_sem.at[g, i], section, ahead(k))
                 for i, k in enumerate((2, 4))] for g in range(2)]
    away = [jnp.logical_or(c != g, mine == 0) for g in range(2)]
    outs = [(remote(made.at[g], result.at[c], o_send.at[g], o_sem.at[c], x * 2 + g, t),
             pltpu.make_async_copy(made.at[g], result.at[c], o_sem.at[c])) for g in range(2)]

    def send_out(g):
        far, near = outs[g]

        @pl.when(away[g])
        def _():
            far.start()

        @pl.when(jnp.logical_not(away[g]))
        def _():
            near.start()

    def first_rows(k, row, n, start):
        base = (HALO, FAR, FAR - ROWS)[k]
        return remote(relay.at[pl.ds(row, n)], ha.at[0, pl.ds(base + start, n)],
                      init_send.at[k], a_sem.at[0, k], c, ahead(k))

    sends = {0: ((1, 0, 128, 0), (2, 80, 48, 80)), 1: [(k, 0, 64, 128) for k in range(3)],
             3: [(k, 0, 64, 192) for k in range(3)]}
    for plane, start, n in shares:
        @pl.when(x == plane)
        def _():
            moved(start, n).wait_recv()
            if plane == 0:
                pltpu.make_async_copy(relay, ha.at[0, pl.ds(HALO, 128)], a_sem.at[0, 0]).start()
            for args in sends[plane]:
                first_rows(*args).start()

    def wait_start(k):
        rows = (pl.ds(HALO, ROWS), pl.ds(FAR, ROWS), pl.ds(0, FAR))[k]
        pltpu.make_async_copy(ha.at[0, rows], ha.at[0, rows], a_sem.at[0, k]).wait()

    seen1 = jnp.where(t >= 1, 1.0, 0.0).astype(jnp.float32)
    seen2 = jnp.where(t >= 2, 1.0, 0.0).astype(jnp.float32)

    def tasks(g, todo):
        for layer, first, last in todo:
            d = SPANS[layer]
            for lo, hi in pieces(first, last):
                at, n = lo + HALO, hi - lo
                if layer == 0:
                    taps = [h0f[pl.ds(at - 2, n), :].astype(jnp.bfloat16),
                            h0f[pl.ds(at - 1, n), :].astype(jnp.bfloat16),
                            ha[g, pl.ds(at, n), :]]
                    before = h0f
                else:
                    src = xb.at[layer - 1]
                    taps = [src[pl.ds(at - 2 * d, n), :], src[pl.ds(at - d, n), :], src[pl.ds(at, n), :]]
                    before = hbuf
                post = dense(taps, g, layer, hi > 0)
                h = before[pl.ds(at, n), :] + post[:, :C]
                hbuf[pl.ds(at, n), :] = h
                for begin, end, seen in ((-HALO, -ROWS, seen2), (-ROWS, 0, seen1), (0, ROWS, None)):
                    i, j = max(begin, lo), min(end, hi)
                    if i >= j:
                        continue
                    part = h[i - lo:j - lo]
                    if seen is not None:
                        part = part * seen
                    else:
                        s = post[i - lo:j - lo, C:]
                        if layer > 0 or g > 0:
                            s = s + sk[pl.ds(i, j - i), :]
                        sk[pl.ds(i, j - i), :] = s
                    if layer < 3:
                        xb[layer, pl.ds(i + HALO, j - i), :] = part.astype(jnp.bfloat16)
                    else:
                        xo[g, pl.ds(i, j - i), :] = part.astype(jnp.bfloat16)

    def last_layer(g):
        for cp in b_copies[g]:
            cp.wait_recv()

        @pl.when(t < 4)
        def _():
            xback[g, 1] = jnp.zeros((ROWS, C), jnp.bfloat16)

        @pl.when(t < 2)
        def _():
            xback[g, 0] = jnp.zeros((ROWS, C), jnp.bfloat16)

        for lo, hi in pieces(0, ROWS):
            rows = pl.ds(lo, hi - lo)
            post = dense([xback[g, 1, rows, :], xback[g, 0, rows, :], xo[g, rows, :]], g, 4, True)
            h = (hbuf[pl.ds(lo + HALO, hi - lo), :] + post[:, :C]).astype(jnp.bfloat16)
            if g == 0:
                ha[1, pl.ds(HALO + lo, hi - lo), :] = h
            else:
                hend[rows, :] = h
            skip = sk[rows, :] + post[:, C:]
            sk[rows, :] = skip
            made[g, 0, rows, :] = h
            made[g, 1, rows, :] = skip.astype(jnp.bfloat16)
        if g == 0:
            for cp in inner[1:]:
                cp.start()
        else:
            @pl.when(x < 3)
            def _():
                for cp in hand:
                    cp.start()

    def widen(g, lo, n):
        h0f[pl.ds(lo, n), :] = ha[g, pl.ds(lo, n), :].astype(jnp.float32)

    for g in range(2):
        def wait_halo(k):
            if g == 0:
                wait_start(k)
            else:
                inner[k].wait_recv()

        for layer in range(LAYERS - 1):
            wait_weights(g, layer)
        if g == 0:
            wait_start(0)
        widen(g, HALO, ROWS)
        tasks(g, OWN)

        wait_halo(1)
        wait_halo(2)
        if g == 0:
            @pl.when(x > 0)
            def _():
                pl.semaphore_signal(taken, inc=1, device_id=(section - 2, tm), device_id_type=MESH)

        @pl.when(t == 0)
        def _():
            ha[g, pl.ds(0, HALO), :] = jnp.zeros((HALO, C), jnp.bfloat16)

        @pl.when(t == 1)
        def _():
            ha[g, pl.ds(0, FAR), :] = jnp.zeros((FAR, C), jnp.bfloat16)

        widen(g, 0, HALO)
        tasks(g, AFTER)
        for cp in b_copies[g]:
            cp.start()
        wait_weights(g, 4)
        if g == 0:
            @pl.when(x > 0)
            def _():
                skip_hand.wait_recv()
                sk[...] += skin[...].astype(jnp.float32)
        last_layer(g)
        if g == 0:
            @pl.when(x == 3)
            def _():
                send_out(0)

    @pl.when(x < 3)
    def _():
        for cp in hand:
            cp.wait_send()
        skip_hand.start()
        skip_hand.wait_send()
        pl.semaphore_wait(taken, 1)
        pl.semaphore_signal(done, inc=1, device_id=(x * 2 + other, tm), device_id_type=MESH)
        pl.semaphore_wait(done, 1)
        send_out(0)

    send_out(1)
    for m in range(2):
        pltpu.make_async_copy(made.at[0], result.at[m], o_sem.at[m]).wait()

    for plane, start, n in shares:
        @pl.when(x == plane)
        def _():
            moved(start, n).wait_send()
            for args in sends[plane]:
                first_rows(*args).wait_send()

    for g in range(2):
        @pl.when(away[g])
        def _():
            outs[g][0].wait_send()

    for cp in w_copies:
        cp.wait_send()
    for cp in inner[1:]:
        cp.wait_send()
    for g in range(2):
        for cp in b_copies[g]:
            cp.wait_send()


def shards(signal, conv_weight, conv_bias, out_weight, out_bias):
    bf16, f32 = jnp.bfloat16, jnp.float32
    any_space = pl.BlockSpec(memory_space=pl.ANY)
    vmem = pl.BlockSpec(memory_space=pltpu.VMEM)
    dma = pltpu.SemaphoreType.DMA
    result = pl.pallas_call(
        kernel,
        out_shape=jax.ShapeDtypeStruct((2, 2, ROWS, C), bf16),
        in_specs=[any_space] * 5,
        out_specs=vmem,
        scratch_shapes=[
            pltpu.VMEM((2, LAYERS, 3 * C, 2 * C), bf16),
            pltpu.VMEM((2, LAYERS, C, 2 * C), bf16),
            pltpu.VMEM((2, LAYERS, 1, 2 * C), f32),
            pltpu.VMEM((2, LAYERS, 1, 2 * C), f32),
            pltpu.VMEM((2, SPAN, C), bf16),
            pltpu.VMEM((SPAN, C), f32),
            pltpu.VMEM((SPAN, C), f32),
            pltpu.VMEM((3, SPAN, C), bf16),
            pltpu.VMEM((2, ROWS, C), bf16),
            pltpu.VMEM((2, 2, ROWS, C), bf16),
            pltpu.VMEM((ROWS, C), bf16),
            pltpu.VMEM((ROWS, C), f32),
            pltpu.VMEM((ROWS, C), bf16),
            pltpu.VMEM((2, 2, ROWS, C), bf16),
            pltpu.VMEM((128, C), bf16),
            dma((12,)), dma((2, 12)),
            dma((3,)), dma((2, 3)),
            dma, dma, dma((3,)),
            dma((2, 2)), dma((2, 2)),
            dma((3,)), dma, dma,
            dma((2,)), dma((2,)),
            pltpu.SemaphoreType.REGULAR, pltpu.SemaphoreType.REGULAR,
        ],
        compiler_params=pltpu.CompilerParams(
            collective_id=0, has_side_effects=True, vmem_limit_bytes=63 * 1024 * 1024),
        cost_estimate=pl.CostEstimate(flops=2 * 2336 * 262144, bytes_accessed=4_000_000, transcendentals=2 * 2336 * 256),
    )(signal, conv_weight, conv_bias.reshape(LAYERS, 1, 2 * C), out_weight, out_bias.reshape(LAYERS, 1, 2 * C))
    return result[None, :, 0], result[None, :, 1].astype(f32)


def solution(mesh):
    return jax.shard_map(
        shards,
        mesh=mesh,
        in_specs=(
            P(None, "tm", None),
            P("section", None, None, None),
            P("section", None, None),
            P("section", None, None, None),
            P("section", None, None),
        ),
        out_specs=(P("section", None, "tm", None), P("section", None, "tm", None)),
        check_vma=False,
    )
```

```python
import jax
import jax.numpy as jnp
from jax import lax
from jax.experimental import pallas as pl
from jax.experimental.pallas import tpu as pltpu
from jax.sharding import PartitionSpec as P

MESH = pl.DeviceIdType.MESH
C = 128
ROWS = 256
NB = 64
FAR = 176
HALO = FAR + ROWS
SPAN = HALO + ROWS
LAYERS = 5
SPANS = (1, 16, 64, 128, 512)
QUARTER = 64
CHUNK = 256
OWN = ((0, 16, ROWS), (1, 48, ROWS), (2, 176, ROWS))
AFTER = ((0, -416, 16), (1, -384, 48), (2, -256, 176), (3, 0, ROWS))


def pieces(lo, hi):
    count = -(-(hi - lo) // CHUNK)
    size = -(-(hi - lo) // (16 * count)) * 16
    return [(at, min(at + size, hi)) for at in range(lo, hi, size)]


def kernel(signal, conv_w, conv_b, out_w, out_b, result,
           wc, wo, bc, bo, ha, h0f, hbuf, xb, xo, xback, hend, sk, skin, made, relay,
           wsend, wsem, a_send, a_sem, r_send, r_sem, init_send, b_send, b_sem, h_send, s_send, s_sem,
           o_send, o_sem, done, taken):
    section = lax.axis_index("section")
    tm = lax.axis_index("tm")
    x, c = section // 2, section % 2
    y, z = tm // 16, tm % 16
    turned = (y + 3 + c) % 4
    pos = z * 4 + (turned ^ (turned >> 1))
    t = jnp.where(c == 1, pos, NB - 1 - pos)
    step = 2 * c - 1

    def tm_of(p, rec):
        n = p % 4
        return (((n ^ (n >> 1)) + 1 - rec) % 4) * 16 + p // 4

    def ahead(k):
        return tm_of((pos + step * k + NB) % NB, c)

    def worker(block, rec):
        return tm_of(jnp.where(rec == 1, block, NB - 1 - block), rec)

    other = 1 - c
    mine = jnp.where(tm == t, 1, 0)

    barrier = pltpu.get_barrier_semaphore()

    def greet(sec, where):
        pl.semaphore_signal(barrier, inc=1, device_id=(sec, where), device_id_type=MESH)

    greet(x * 2 + other, tm)
    for k in (1, 2, 4):
        greet(section, ahead(-k))

    @pl.when(x > 0)
    def _():
        for k in range(3):
            greet(section - 2, ahead(-k))

    greet(x * 2 + other, t)

    @pl.when(x == 0)
    def _():
        for plane in range(4):
            for k in range(3):
                if plane > 0 or k == 1:
                    greet(plane * 2 + c, ahead(-k))

    for m in range(2):
        @pl.when(jnp.logical_or(c != m, tm != worker(tm, m)))
        def _():
            greet(x * 2 + m, worker(tm, m))

    pl.semaphore_wait(barrier, 7 - mine + jnp.where(x < 3, 3, 0) + jnp.where(x == 0, 1, 3))

    def remote(src, dst, send, recv, sec, where):
        return pltpu.make_async_remote_copy(
            src_ref=src, dst_ref=dst, send_sem=send, recv_sem=recv,
            device_id=(sec, where), device_id_type=MESH)

    quarter = remote(signal.at[other, pl.ds(pl.multiple_of(x * QUARTER, QUARTER), QUARTER)], relay, r_send, r_sem,
                     x * 2 + other, worker(tm, other))
    quarter.start()

    parts = ((0, ROWS, HALO), (0, ROWS, FAR), (ROWS - FAR, FAR, 0))

    def start_copies(g, src, sends, sec):
        return [remote(src.at[pl.ds(lo, n)], ha.at[g, pl.ds(at, n)], sends.at[k], a_sem.at[g, k], sec, ahead(k))
                for k, (lo, n, at) in enumerate(parts)]

    jobs = []
    for layer in range(LAYERS):
        jobs.append((conv_w.at[0, layer], lambda g, l=layer: wc.at[g, l]))
        jobs.append((out_w.at[0, layer], lambda g, l=layer: wo.at[g, l]))
        if layer == 0:
            jobs.append((conv_b, lambda g: bc.at[g]))
            jobs.append((out_b, lambda g: bo.at[g]))
    w_copies = []
    for i, (src, dst) in enumerate(jobs):
        cp = remote(src, dst(c), wsend.at[i], wsem.at[c, i], x * 2 + other, tm)
        cp.start()
        w_copies.append(cp)
        pltpu.make_async_copy(src, dst(c), wsem.at[c, i]).start()
    need = {0: (0, 1, 2, 3), 1: (4, 5), 2: (6, 7), 3: (8, 9), 4: (10, 11)}

    def wait_weights(g, layer):
        for i in need[layer]:
            src, dst = jobs[i]
            pltpu.make_async_copy(src, dst(g), wsem.at[g, i]).wait()

    def dense(taps, g, layer, own):
        pre = jnp.dot(jnp.concatenate(taps, axis=1), wc[g, layer],
                      preferred_element_type=jnp.float32) + bc[g, layer]
        pre = pre.astype(jnp.bfloat16)
        half = jnp.bfloat16(0.5)
        gated = jnp.tanh(pre[:, :C]) * (half * jnp.tanh(half * pre[:, C:]) + half)
        if own:
            return jnp.dot(gated, wo[g, layer], preferred_element_type=jnp.float32) + bo[g, layer]
        return (jnp.dot(gated, wo[g, layer, :, pl.ds(0, C)], preferred_element_type=jnp.float32)
                + bo[g, layer, :, pl.ds(0, C)])

    next_section = jnp.where(x < 3, section + 2, section - 6)
    hand = start_copies(0, hend, h_send, next_section)
    skip_hand = remote(made.at[1, 1], skin, s_send, s_sem, next_section, ahead(0))
    inner = start_copies(1, ha.at[1, pl.ds(HALO, ROWS)], a_send, section)
    b_copies = [[remote(xo.at[g], xback.at[g, i], b_send.at[g, i], b_sem.at[g, i], section, ahead(k))
                 for i, k in enumerate((2, 4))] for g in range(2)]
    away = [jnp.logical_or(c != g, mine == 0) for g in range(2)]
    outs = [(remote(made.at[g], result.at[c], o_send.at[g], o_sem.at[c], x * 2 + g, t),
             pltpu.make_async_copy(made.at[g], result.at[c], o_sem.at[c])) for g in range(2)]

    def send_out(g):
        far, near = outs[g]

        @pl.when(away[g])
        def _():
            far.start()

        @pl.when(jnp.logical_not(away[g]))
        def _():
            near.start()

    def first_rows(k, row, n, start):
        base = (HALO, FAR, FAR - ROWS)[k]
        return remote(relay.at[pl.ds(row, n)], ha.at[0, pl.ds(pl.multiple_of(base + start, 16), n)],
                      init_send.at[k], a_sem.at[0, k], c, ahead(k))

    first = x * QUARTER
    quarter.wait_recv()

    @pl.when(x == 0)
    def _():
        pltpu.make_async_copy(relay, ha.at[0, pl.ds(HALO, QUARTER)], a_sem.at[0, 0]).start()
        first_rows(1, 0, QUARTER, 0).start()

    @pl.when(x > 0)
    def _():
        first_rows(0, 0, QUARTER, first).start()
        first_rows(1, 0, QUARTER, first).start()

    @pl.when(x == 1)
    def _():
        first_rows(2, 16, QUARTER - 16, QUARTER + 16).start()

    @pl.when(x > 1)
    def _():
        first_rows(2, 0, QUARTER, first).start()

    def wait_start(k):
        rows = (pl.ds(HALO, ROWS), pl.ds(FAR, ROWS), pl.ds(0, FAR))[k]
        pltpu.make_async_copy(ha.at[0, rows], ha.at[0, rows], a_sem.at[0, k]).wait()

    seen1 = jnp.where(t >= 1, 1.0, 0.0).astype(jnp.float32)
    seen2 = jnp.where(t >= 2, 1.0, 0.0).astype(jnp.float32)

    def tasks(g, todo):
        for layer, first, last in todo:
            d = SPANS[layer]
            for lo, hi in pieces(first, last):
                at, n = lo + HALO, hi - lo
                if layer == 0:
                    taps = [h0f[pl.ds(at - 2, n), :].astype(jnp.bfloat16),
                            h0f[pl.ds(at - 1, n), :].astype(jnp.bfloat16),
                            ha[g, pl.ds(at, n), :]]
                    before = h0f
                else:
                    src = xb.at[layer - 1]
                    taps = [src[pl.ds(at - 2 * d, n), :], src[pl.ds(at - d, n), :], src[pl.ds(at, n), :]]
                    before = hbuf
                post = dense(taps, g, layer, hi > 0)
                h = before[pl.ds(at, n), :] + post[:, :C]
                hbuf[pl.ds(at, n), :] = h
                for begin, end, seen in ((-HALO, -ROWS, seen2), (-ROWS, 0, seen1), (0, ROWS, None)):
                    i, j = max(begin, lo), min(end, hi)
                    if i >= j:
                        continue
                    part = h[i - lo:j - lo]
                    if seen is not None:
                        part = part * seen
                    else:
                        s = post[i - lo:j - lo, C:]
                        if layer > 0 or g > 0:
                            s = s + sk[pl.ds(i, j - i), :]
                        sk[pl.ds(i, j - i), :] = s
                    if layer < 3:
                        xb[layer, pl.ds(i + HALO, j - i), :] = part.astype(jnp.bfloat16)
                    else:
                        xo[g, pl.ds(i, j - i), :] = part.astype(jnp.bfloat16)

    def last_layer(g):
        for cp in b_copies[g]:
            cp.wait_recv()

        @pl.when(t < 4)
        def _():
            xback[g, 1] = jnp.zeros((ROWS, C), jnp.bfloat16)

        @pl.when(t < 2)
        def _():
            xback[g, 0] = jnp.zeros((ROWS, C), jnp.bfloat16)

        for lo, hi in pieces(0, ROWS):
            rows = pl.ds(lo, hi - lo)
            post = dense([xback[g, 1, rows, :], xback[g, 0, rows, :], xo[g, rows, :]], g, 4, True)
            h = (hbuf[pl.ds(lo + HALO, hi - lo), :] + post[:, :C]).astype(jnp.bfloat16)
            if g == 0:
                ha[1, pl.ds(HALO + lo, hi - lo), :] = h
            else:
                hend[rows, :] = h
            skip = sk[rows, :] + post[:, C:]
            sk[rows, :] = skip
            made[g, 0, rows, :] = h
            made[g, 1, rows, :] = skip.astype(jnp.bfloat16)
        if g == 0:
            for cp in inner[1:]:
                cp.start()
        else:
            @pl.when(x < 3)
            def _():
                for cp in hand:
                    cp.start()

    def widen(g, lo, n):
        h0f[pl.ds(lo, n), :] = ha[g, pl.ds(lo, n), :].astype(jnp.float32)

    for g in range(2):
        def wait_halo(k):
            if g == 0:
                wait_start(k)
            else:
                inner[k].wait_recv()

        for layer in range(LAYERS - 1):
            wait_weights(g, layer)
        if g == 0:
            wait_start(0)
        widen(g, HALO, ROWS)
        tasks(g, OWN)

        wait_halo(1)
        wait_halo(2)
        if g == 0:
            @pl.when(x > 0)
            def _():
                pl.semaphore_signal(taken, inc=1, device_id=(section - 2, tm), device_id_type=MESH)
        else:
            @pl.when(x == 3)
            def _():
                send_out(0)

        @pl.when(t == 0)
        def _():
            ha[g, pl.ds(0, HALO), :] = jnp.zeros((HALO, C), jnp.bfloat16)

        @pl.when(t == 1)
        def _():
            ha[g, pl.ds(0, FAR), :] = jnp.zeros((FAR, C), jnp.bfloat16)

        widen(g, 0, HALO)
        tasks(g, AFTER)
        for cp in b_copies[g]:
            cp.start()
        wait_weights(g, 4)
        if g == 0:
            @pl.when(x > 0)
            def _():
                skip_hand.wait_recv()
                sk[...] += skin[...].astype(jnp.float32)
        last_layer(g)

    @pl.when(x < 3)
    def _():
        for cp in hand:
            cp.wait_send()
        skip_hand.start()
        skip_hand.wait_send()
        pl.semaphore_wait(taken, 1)
        pl.semaphore_signal(done, inc=1, device_id=(x * 2 + other, tm), device_id_type=MESH)
        pl.semaphore_wait(done, 1)
        send_out(0)

    send_out(1)
    for m in range(2):
        pltpu.make_async_copy(made.at[0], result.at[m], o_sem.at[m]).wait()

    quarter.wait_send()

    @pl.when(x > 0)
    def _():
        first_rows(0, 0, QUARTER, first).wait_send()

    first_rows(1, 0, QUARTER, first).wait_send()

    @pl.when(x == 1)
    def _():
        first_rows(2, 16, QUARTER - 16, QUARTER + 16).wait_send()

    @pl.when(x > 1)
    def _():
        first_rows(2, 0, QUARTER, first).wait_send()

    for g in range(2):
        @pl.when(away[g])
        def _():
            outs[g][0].wait_send()

    for cp in w_copies:
        cp.wait_send()
    for cp in inner[1:]:
        cp.wait_send()
    for g in range(2):
        for cp in b_copies[g]:
            cp.wait_send()


def shards(signal, conv_weight, conv_bias, out_weight, out_bias):
    bf16, f32 = jnp.bfloat16, jnp.float32
    any_space = pl.BlockSpec(memory_space=pl.ANY)
    vmem = pl.BlockSpec(memory_space=pltpu.VMEM)
    dma = pltpu.SemaphoreType.DMA
    result = pl.pallas_call(
        kernel,
        out_shape=jax.ShapeDtypeStruct((2, 2, ROWS, C), bf16),
        in_specs=[any_space] * 5,
        out_specs=vmem,
        scratch_shapes=[
            pltpu.VMEM((2, LAYERS, 3 * C, 2 * C), bf16),
            pltpu.VMEM((2, LAYERS, C, 2 * C), bf16),
            pltpu.VMEM((2, LAYERS, 1, 2 * C), f32),
            pltpu.VMEM((2, LAYERS, 1, 2 * C), f32),
            pltpu.VMEM((2, SPAN, C), bf16),
            pltpu.VMEM((SPAN, C), f32),
            pltpu.VMEM((SPAN, C), f32),
            pltpu.VMEM((3, SPAN, C), bf16),
            pltpu.VMEM((2, ROWS, C), bf16),
            pltpu.VMEM((2, 2, ROWS, C), bf16),
            pltpu.VMEM((ROWS, C), bf16),
            pltpu.VMEM((ROWS, C), f32),
            pltpu.VMEM((ROWS, C), bf16),
            pltpu.VMEM((2, 2, ROWS, C), bf16),
            pltpu.VMEM((QUARTER, C), bf16),
            dma((12,)), dma((2, 12)),
            dma((3,)), dma((2, 3)),
            dma, dma, dma((3,)),
            dma((2, 2)), dma((2, 2)),
            dma((3,)), dma, dma,
            dma((2,)), dma((2,)),
            pltpu.SemaphoreType.REGULAR, pltpu.SemaphoreType.REGULAR,
        ],
        compiler_params=pltpu.CompilerParams(
            collective_id=0, has_side_effects=True, vmem_limit_bytes=63 * 1024 * 1024),
        cost_estimate=pl.CostEstimate(flops=2 * 2336 * 262144, bytes_accessed=4_000_000, transcendentals=2 * 2336 * 256),
    )(signal, conv_weight, conv_bias.reshape(LAYERS, 1, 2 * C), out_weight, out_bias.reshape(LAYERS, 1, 2 * C))
    return result[None, :, 0], result[None, :, 1].astype(f32)


def solution(mesh):
    return jax.shard_map(
        shards,
        mesh=mesh,
        in_specs=(
            P(None, "tm", None),
            P("section", None, None, None),
            P("section", None, None),
            P("section", None, None, None),
            P("section", None, None),
        ),
        out_specs=(P("section", None, "tm", None), P("section", None, "tm", None)),
        check_vma=False,
    )
```
